32 devices in a mesh: dp: 2 (over x), seq: 16 (over z, y, core).
Axes of the slice: x: 2, y: 2, z: 4, core: 2. Of those that a mesh axis runs over, the one named last changes fastest.
Arguments:
- queries: bfloat16 [2, 2048, 2048], P('dp', 'seq'), may hold values from -6 to 6
- keys: bfloat16 [2, 2048, 2048], P('dp', 'seq'), may hold values from -0.75 to 0.75
- values: bfloat16 [2, 2048, 2048], P('dp', 'seq'), may hold values from -6 to 6
- log_decay: float32 [2, 32, 2048], P('dp', None, 'seq'), may hold values from -0.7 to 0
- gain: float32 [2048], replicated, may hold values from 0.25 to 1.75
- d_out: bfloat16 [2, 2048, 2048], P('dp', 'seq'), may hold values from -12 to 12
Outputs:
- d_queries: bfloat16 [2, 2048, 2048], P('dp', 'seq')
- d_keys: bfloat16 [2, 2048, 2048], P('dp', 'seq')
- d_values: bfloat16 [2, 2048, 2048], P('dp', 'seq')
- d_log_decay: float32 [2, 32, 2048], P('dp', None, 'seq')
- d_gain: float32 [2048], replicated
The draws below stay inside these ranges and needn't reach their ends.
All inputs are finite; a program needn't handle non-finite values.
Results may differ from the reference program's by a relative error of at most 0.001.
Values sent between devices are 32-bit elements; how exact they have to be, the bound alone decides.
A program may use at most 192 MiB of HBM per device.

```python
import math
import jax
import jax.numpy as jnp
from jax import lax

ATTENTION_HEADS = 32
HEAD = 64
TOK_DEV = 128
SEQUENCE_LENGTH = 2048
BATCH_SEQUENCES = 2
N_SEQ = 16


def draw_log_decay(key, part):
    random_key_variety, random_key_gradual, random_key_quick, random_key_coarse, random_key_location, random_key_spike = jax.random.split(key, 6)
    kind = jax.random.randint(random_key_variety, (1, ATTENTION_HEADS, 1), 0, 2) > 0
    slow = jnp.exp(jax.random.uniform(random_key_gradual, (1, ATTENTION_HEADS, 1), jnp.float32, math.log(0.05), math.log(0.3))) / SEQUENCE_LENGTH
    fast = jnp.exp(jax.random.uniform(random_key_quick, (1, ATTENTION_HEADS, 1), jnp.float32, math.log(0.02), math.log(0.033)))
    decay_speed = jnp.where(kind, slow, fast)
    coarse_values = jnp.exp(jax.random.uniform(random_key_coarse, (BATCH_SEQUENCES, ATTENTION_HEADS, SEQUENCE_LENGTH), jnp.float32, math.log(0.5), math.log(2.0)))
    places = jax.random.randint(random_key_location, (BATCH_SEQUENCES, ATTENTION_HEADS, 2), 0, SEQUENCE_LENGTH)
    spots = jnp.arange(SEQUENCE_LENGTH)[None, None, :, None] == places[:, :, None, :]
    hit_positions = jnp.any(spots, axis=3)
    sudden_spike = jnp.log(jax.random.uniform(random_key_spike, (BATCH_SEQUENCES, ATTENTION_HEADS, SEQUENCE_LENGTH), jnp.float32, 0.5, 0.8))
    return jnp.where(hit_positions, sudden_spike, -decay_speed * coarse_values).astype(jnp.float32)


def draw_d_out(key, part):
    key_base = jax.random.fold_in(key, 0)
    ramp = 1.0 + 2.0 * jnp.arange(SEQUENCE_LENGTH, dtype=jnp.float32)[None, :, None] / SEQUENCE_LENGTH
    base = jax.random.normal(key_base, (BATCH_SEQUENCES, SEQUENCE_LENGTH, ATTENTION_HEADS * HEAD), jnp.float32)
    return (jnp.clip(base, -4.0, 4.0) * ramp).astype(jnp.bfloat16)


def block_scale(stream_key, shape, cuts, low, largest):
    def one(dim, blocks):
        steps = jax.random.uniform(jax.random.fold_in(jax.random.fold_in(stream_key, 6), dim), (blocks,), jnp.float32, low / len(cuts), largest / len(cuts))
        return jnp.repeat(jnp.exp(steps), shape[dim] // blocks).reshape((-1,) + (1,) * (len(shape) - dim - 1))

    level = one(*cuts[0])
    for cut in cuts[1:]:
        level = level * one(*cut)
    return level


def scatter_about(key, extent, scale, reach, pieces=(), kind=jnp.bfloat16):
    result = jax.random.normal(key, extent, jnp.float32) * scale
    if len(pieces) > 0:
        result = block_scale(key, extent, pieces, -0.22, 0.18) * result
    return jnp.clip(result, min=-reach, max=reach).astype(kind)


def setup_inputs(seed: int = 0) -> dict:
    arg_keys = jax.random.split(jax.random.key(seed), 7)
    return {
        "queries": scatter_about(arg_keys[0], (BATCH_SEQUENCES, SEQUENCE_LENGTH, ATTENTION_HEADS * HEAD), 1.0, 6.0, ((0, 2), (1, 16))),
        "keys": scatter_about(arg_keys[1], (BATCH_SEQUENCES, SEQUENCE_LENGTH, ATTENTION_HEADS * HEAD), HEAD ** -0.5, 0.75, ((0, 2), (1, 16))),
        "values": scatter_about(arg_keys[2], (BATCH_SEQUENCES, SEQUENCE_LENGTH, ATTENTION_HEADS * HEAD), 1.0, 6.0, ((0, 2), (1, 16))),
        "log_decay": draw_log_decay(jax.random.fold_in(arg_keys[6], 71), 0),
        "gain": jnp.clip(1.0 + 0.15 * jax.random.normal(arg_keys[4], (ATTENTION_HEADS * HEAD,), jnp.float32), 0.25, 1.75),
        "d_out": draw_d_out(jax.random.fold_in(arg_keys[6], 71), 0),
    }


HIGH = lax.Precision.HIGHEST
EPSILON = 1e-06

def decay_table(log_block):
    cumulative = jnp.cumsum(log_block, axis=1)
    spread = cumulative[:, :, None] - cumulative[:, None, :]
    length = log_block.shape[1]
    lower = jnp.arange(length)[:, None] >= jnp.arange(length)[None, :]
    table = jnp.where(lower[None], jnp.exp(jnp.minimum(spread, 0.0)), 0.0)
    return (cumulative, table)

def block_out(query, keys, values, log_block, start_state):
    cumulative, table = decay_table(log_block)
    scores = jnp.einsum('htd,hsd->hts', query, keys, precision=HIGH) * table
    inside = jnp.einsum('hts,hse->hte', scores, values, precision=HIGH)
    carried = jnp.einsum('htd,hde->hte', query, start_state, precision=HIGH)
    return inside + jnp.exp(cumulative)[:, :, None] * carried

def block_end(keys, values, log_block, start_state):
    cumulative = jnp.cumsum(log_block, axis=1)
    total = cumulative[:, -1]
    weighted = keys * jnp.exp(total[:, None] - cumulative)[:, :, None]
    fresh = jnp.einsum('hsd,hse->hde', weighted, values, precision=HIGH)
    return jnp.exp(total)[:, None, None] * start_state + fresh

def normalize(attended, gain):
    heads, length, width = attended.shape
    flat = jnp.transpose(attended, (1, 0, 2)).reshape(length, heads * width)
    scale = jnp.sqrt(lax.optimization_barrier(jnp.mean(flat * flat, axis=1, keepdims=True)) + EPSILON)
    return flat / scale * gain

def forward(query, keys, values, log_decay, gain):

    def advance(state, item):
        query_block, key_block, value_block, log_block = item
        attended = block_out(query_block, key_block, value_block, log_block, state)
        return (block_end(key_block, value_block, log_block, state), normalize(attended, gain))
    start = jnp.zeros((ATTENTION_HEADS, HEAD, HEAD), jnp.float32)
    _, normed = lax.scan(advance, start, (query, keys, values, log_decay))
    return normed

def to_heads(array):
    shaped = array.astype(jnp.float32).reshape(N_SEQ, TOK_DEV, ATTENTION_HEADS, HEAD)
    return jnp.transpose(shaped, (0, 2, 1, 3))

def from_heads(array):
    return jnp.transpose(array, (0, 2, 1, 3)).reshape(N_SEQ * TOK_DEV, ATTENTION_HEADS * HEAD).astype(jnp.bfloat16)

def reference(queries, keys, values, log_decay, gain, d_out):

    def one_sequence(item):
        query, key_seq, value_seq, log_seq, cotangent = item
        log_blocks = jnp.transpose(log_seq.reshape(ATTENTION_HEADS, N_SEQ, TOK_DEV), (1, 0, 2))
        _, pull = jax.vjp(forward, to_heads(query), to_heads(key_seq), to_heads(value_seq), log_blocks, gain)
        grads = pull(cotangent.astype(jnp.float32).reshape(N_SEQ, TOK_DEV, ATTENTION_HEADS * HEAD))
        d_log = jnp.transpose(grads[3], (1, 0, 2)).reshape(ATTENTION_HEADS, N_SEQ * TOK_DEV)
        return (from_heads(grads[0]), from_heads(grads[1]), from_heads(grads[2]), d_log, grads[4])
    d_queries, d_keys, d_values, d_log_decay, gains = lax.map(one_sequence, (queries, keys, values, log_decay, d_out))
    return (d_queries, d_keys, d_values, d_log_decay, lax.optimization_barrier(jnp.sum(gains, axis=0)))
```

```python
import functools

import jax
import jax.numpy as jnp
from jax import lax
from jax.experimental import pallas as pl
from jax.experimental.pallas import tpu as pltpu
from jax.sharding import PartitionSpec as P

EPSILON = 1e-06
HIGH = lax.Precision.HIGHEST
F32 = jnp.float32
BF16 = jnp.bfloat16
UNROLL = 2


def dot(a, b, contract, precision=None):
    return lax.dot_general(
        a, b, (contract, ((), ())), precision=precision, preferred_element_type=F32
    )


def nn(a, b, precision=None):
    return dot(a, b, ((1,), (0,)), precision)


def nt(a, b, precision=None):
    return dot(a, b, ((1,), (1,)), precision)


def tn(a, b):
    return dot(a, b, ((0,), (0,)))


def split(x):
    high = x.astype(BF16)
    return high, (x - high.astype(F32)).astype(BF16)


def rows(*parts):
    return jnp.concatenate(parts, axis=0)


def lanes(*parts):
    return jnp.concatenate(parts, axis=1)


def kernel(
    size,
    width,
    q_ref, k_ref, v_ref, log_ref, gain_ref, do_ref,
    dq_ref, dk_ref, dv_ref, dlog_ref, dgain_ref,
    scratch,
):
    s = scratch
    seq_size, dp_size, levels = size
    length = q_ref.shape[0]
    pair_width = 2 * width
    pairs = q_ref.shape[1] // pair_width
    heads = 2 * pairs
    group = 2 ** levels
    chain = seq_size // group
    me = lax.axis_index("seq")
    dp = lax.axis_index("dp")

    def at_seq(index):
        return {"seq": index}

    def bit_of(value, level):
        return lax.rem(lax.div(value, 2 ** level), 2)

    def flipped(value, level):
        return value + 2 ** level * (1 - 2 * bit_of(value, level))

    place = lax.div(me, group)
    after = lax.rem(me + group, seq_size)
    before = lax.rem(me + seq_size - group, seq_size)
    seq_bits = seq_size.bit_length() - 1
    dp_bits = dp_size.bit_length() - 1
    partners = [at_seq(flipped(me, level)) for level in range(seq_bits)]
    partners += [{"dp": flipped(dp, level)} for level in range(dp_bits)]
    greeted = partners + [at_seq(after), at_seq(before)]

    barrier = pltpu.get_barrier_semaphore()
    for other in greeted:
        pl.semaphore_signal(
            barrier, inc=1, device_id=other, device_id_type=pl.DeviceIdType.MESH
        )

    def copy_to(source, target, send, recv, device):
        return pltpu.make_async_remote_copy(
            src_ref=source, dst_ref=target, send_sem=send, recv_sem=recv,
            device_id=device, device_id_type=pl.DeviceIdType.MESH,
        )

    lane_row = lax.broadcasted_iota(jnp.int32, (1, pair_width), 1)
    low_row = lane_row < width

    def low(shape):
        return lax.broadcasted_iota(jnp.int32, shape, 1) < width

    low_tok = low((length, pair_width))
    low_state = low((width, pair_width))

    def columns(pair):
        if isinstance(pair, int):
            return pl.ds(pair * pair_width, pair_width)
        return pl.ds(pl.multiple_of(pair * pair_width, pair_width), pair_width)

    def stacked(block):
        zero = jnp.zeros_like(block)
        return rows(jnp.where(low_tok, block, zero), jnp.where(low_tok, zero, block))

    def diagonal(state):
        zero = jnp.zeros_like(state)
        return rows(jnp.where(low_state, state, zero), jnp.where(low_state, zero, state))

    def packed(square):
        return jnp.where(low_state, square[:width], square[width:])

    def picked(tall):
        return jnp.where(low_tok, tall[:length], tall[length:])

    def each(start, stop, compute):
        step = UNROLL if (stop - start) % UNROLL == 0 else 1

        def body(index, carry):
            stores = []
            for offset in range(step):
                stores += compute(start + index * step + offset)
            for ref, where, value in stores:
                ref[where] = value
            return carry

        lax.fori_loop(0, (stop - start) // step, body, 0)

    ones_from = lax.broadcasted_iota(jnp.int32, (length, length), 0)
    ones_to = lax.broadcasted_iota(jnp.int32, (length, length), 1)
    causal = ones_from >= ones_to
    log_block = log_ref[...]
    s.cum[...] = nn(log_block, (ones_from <= ones_to).astype(F32), HIGH)
    cum_columns = nt(causal.astype(F32), log_block, HIGH)

    for pair in range(pairs):
        first = jnp.broadcast_to(cum_columns[:, 2 * pair:2 * pair + 1], (length, length))
        second = jnp.broadcast_to(cum_columns[:, 2 * pair + 1:2 * pair + 2], (length, length))
        s.spread[2 * pair] = first
        s.spread[2 * pair + 1] = second
        mixed = jnp.where(low_tok, first, second)
        total = mixed[length - 1:length, :]
        s.grow[pair] = jnp.exp(mixed)
        late = jnp.exp(total - mixed)
        s.late[pair] = late
        s.decay[0, pair:pair + 1, :] = jnp.exp(total)
        key = k_ref[:, columns(pair)]
        value = v_ref[:, columns(pair)].astype(F32) * late
        high, rest = split(value)
        s.fresh[pair] = packed(tn(rows(key, key), rows(high, rest)))

    pl.semaphore_wait(barrier, len(greeted))

    def scan(name, source, result, backward, works):
        x = s.scans[name]
        first_bit = 1 if backward else 0
        current, base, count = source, 0, pairs
        infos = []
        for level in range(levels):
            bit = bit_of(me, level)
            half = count // 2
            keep, give = bit * half, (1 - bit) * half
            partner = at_seq(flipped(me, level))
            copies = [
                copy_to(
                    current.at[pl.ds(give, half)], x.received[level],
                    x.up_send.at[level], x.up_recv.at[level], partner,
                )
            ]
            if not backward:
                copies.append(
                    copy_to(
                        s.decay.at[level], s.decay_other.at[level],
                        s.decay_send.at[level], s.decay_recv.at[level], partner,
                    )
                )
            for copy in copies:
                copy.start()
            works[level]()
            for copy in copies:
                copy.wait()
            if not backward:
                s.decay[level + 1] = s.decay[level] * s.decay_other[level]
            mine_first = jnp.broadcast_to(bit, (width, pair_width)) == first_bit
            mine_first_row = jnp.broadcast_to(bit, (1, pair_width)) == first_bit
            for i in range(half):
                own = current[keep + i]
                other = x.received[level][i]
                row = pl.ds(base + keep + i, 1)
                own_decay = s.decay[level, row, :]
                other_decay = s.decay_other[level, row, :]
                earlier = jnp.where(mine_first, own, other)
                later = jnp.where(mine_first, other, own)
                later_decay = jnp.where(mine_first_row, other_decay, own_decay)
                x.first[level][i] = earlier
                x.total[level][i] = later_decay * earlier + later
            infos.append((bit, half, keep, base, partner, mine_first, mine_first_row))
            current, base, count = x.total[level], base + keep, half

        start_place = chain - 1 if backward else 0
        stop_place = 0 if backward else chain - 1
        target = at_seq(before if backward else after)
        works[levels]()

        def link(i):
            return copy_to(
                x.chain_out.at[i], x.chain_in.at[i],
                x.chain_send.at[i], x.chain_recv.at[i], target,
            )

        @pl.when(place == start_place)
        def _():
            x.chain_in[...] = jnp.zeros_like(x.chain_in)

        for i in range(count):
            @pl.when(place != start_place)
            def _(i=i):
                link(i).wait_recv()

            @pl.when(place != stop_place)
            def _(i=i):
                row = pl.ds(base + i, 1)
                x.chain_out[i] = s.decay[levels, row, :] * x.chain_in[i] + current[i]
                link(i).start()

        prefix = x.chain_in
        for level in reversed(range(levels)):
            bit, half, keep, base, partner, mine_first, mine_first_row = infos[level]
            out = x.prefix[level] if level > 0 else result
            for i in range(half):
                row = pl.ds(base + keep + i, 1)
                own_decay = s.decay[level, row, :]
                other_decay = s.decay_other[level, row, :]
                first_decay = jnp.where(mine_first_row, own_decay, other_decay)
                given = prefix[i]
                moved = first_decay * given + x.first[level][i]
                x.give[level][i] = jnp.where(mine_first, moved, given)
                out[keep + i] = jnp.where(mine_first, given, moved)
            copy = copy_to(
                x.give[level], out.at[pl.ds(keep, half)],
                x.down_send.at[level], x.down_recv.at[level], partner,
            )
            copy.start()
            works[levels + 1 + levels - 1 - level]()
            copy.wait()
            prefix = out

        @pl.when(place != stop_place)
        def _():
            for i in range(count):
                link(i).wait_send()

    def inside(pair):
        query = q_ref[:, columns(pair)]
        scores = nt(query, stacked(k_ref[:, columns(pair)]))
        tables = []
        for head in range(2):
            gap = s.spread[2 * pair + head] - s.cum[pl.ds(2 * pair + head, 1), :]
            tables.append(jnp.where(causal, jnp.exp(jnp.minimum(gap, 0.0)), 0.0))
        table = lanes(*tables)
        high, rest = split(scores * table)
        values = stacked(v_ref[:, columns(pair)])
        part = nn(lanes(high, rest), rows(values, values))
        return [
            (s.table, pair, table), (s.score_high, pair, high),
            (s.score_rest, pair, rest), (s.attended, pair, part),
        ]

    def nothing():
        pass

    def cut(shares, compute):
        works, start = [], 0
        for share in shares:
            stop = min(pairs, start + share)
            if stop > start:
                works.append(functools.partial(each, start, stop, compute))
            else:
                works.append(nothing)
            start = stop
        assert start == pairs
        return works

    def shares(early, late):
        counts = [early] + [late] * (levels - 1)
        return counts + [pairs - sum(counts)] + [0] * levels

    scan("forward", s.fresh, s.start, False, cut(shares(4, 6), inside))

    s.squares[...] = jnp.zeros_like(s.squares)
    s.products[...] = jnp.zeros_like(s.products)

    def attend(pair):
        query = q_ref[:, columns(pair)]
        high, rest = split(diagonal(s.start[pair]))
        carried = nn(lanes(query, query), rows(high, rest))
        attended = s.attended[pair] + s.grow[pair] * carried
        slope = do_ref[:, columns(pair)].astype(F32) * gain_ref[pl.ds(pair, 1), :]
        return attended, slope

    def attend_pairs(index, carry):
        squares, products = s.squares[...], s.products[...]
        for offset in range(UNROLL):
            pair = index * UNROLL + offset
            attended, slope = attend(pair)
            s.attended[pair] = attended
            squares = squares + attended * attended
            products = products + attended * slope
        s.squares[...] = squares
        s.products[...] = products
        return carry

    lax.fori_loop(0, pairs // UNROLL, attend_pairs, 0)
    features = pairs * pair_width
    mean = jnp.sum(s.squares[...], axis=1, keepdims=True) / features
    inverse = 1.0 / jnp.sqrt(mean + EPSILON)
    weight = jnp.sum(s.products[...], axis=1, keepdims=True) / features * inverse * inverse * inverse
    s.inverse[...] = jnp.broadcast_to(inverse, (length, pair_width))
    s.weight[...] = jnp.broadcast_to(weight, (length, pair_width))

    def slopes(pair):
        cotangent = do_ref[:, columns(pair)].astype(F32)
        attended = s.attended[pair]
        inverse = s.inverse[...]
        gained = jnp.sum(attended * inverse * cotangent, axis=0, keepdims=True)
        slope = cotangent * gain_ref[pl.ds(pair, 1), :] * inverse - attended * s.weight[...]
        high, rest = split(slope)
        grown_high, grown_rest = split(slope * s.grow[pair])
        query = q_ref[:, columns(pair)]
        incoming = packed(tn(rows(query, query), rows(grown_high, grown_rest)))
        return [
            (s.slope_high, pair, high), (s.slope_rest, pair, rest),
            (s.incoming, pair, incoming),
            (s.gained, (0, pl.ds(pair, 1), slice(None)), gained),
        ]

    each(0, pairs, slopes)

    def gain_step(step):
        copy = copy_to(
            s.gained.at[step], s.gained_other.at[step],
            s.gain_send.at[step], s.gain_recv.at[step], partners[step],
        )
        return copy

    def gain_advance(step):
        gain_step(step).wait()
        s.gained[step + 1] = s.gained[step] + s.gained_other[step]
        if step + 1 < len(partners):
            gain_step(step + 1).start()

    gain_step(0).start()

    def grads(pair):
        query, key = q_ref[:, columns(pair)], k_ref[:, columns(pair)]
        keys, values = stacked(key), stacked(v_ref[:, columns(pair)])
        high, rest = s.slope_high[pair], s.slope_rest[pair]
        from_values = nt(lanes(high, rest), lanes(values, values))
        inner_high, inner_rest = split(from_values * s.table[pair])
        state_high, state_rest = split(diagonal(s.start[pair]))
        carried = nt(lanes(high, rest, high), lanes(state_high, state_high, state_rest))
        d_query = nn(lanes(inner_high, inner_rest), rows(keys, keys)) + s.grow[pair] * carried
        d_key = picked(tn(rows(inner_high, inner_rest), rows(query, query)))
        score_high, score_rest = s.score_high[pair], s.score_rest[pair]
        d_value = picked(tn(rows(score_high, score_rest, score_high), rows(high, high, rest)))
        return [
            (dq_ref, (slice(None), columns(pair)), d_query.astype(BF16)),
            (s.query_part, pair, d_query * query.astype(F32)),
            (s.d_key, pair, d_key), (s.d_value, pair, d_value),
        ]

    works = cut(shares(4, 6), grads)
    steps = len(partners)
    pieces = [(steps * i // len(works), steps * (i + 1) // len(works)) for i in range(len(works))]

    def with_gain(work, piece):
        def run():
            work()
            for step in range(*piece):
                gain_advance(step)
        return run

    scan("backward", s.incoming, s.end, True, [with_gain(*both) for both in zip(works, pieces)])
    dgain_ref[...] = s.gained[steps]

    s.d_cum[...] = jnp.zeros_like(s.d_cum)
    last = lax.broadcasted_iota(jnp.int32, (length, pair_width), 0) == length - 1
    head_of = lax.broadcasted_iota(jnp.int32, (heads, pair_width), 0)
    side_of = lax.broadcasted_iota(jnp.int32, (heads, pair_width), 1)

    def finish(pair):
        key, value = k_ref[:, columns(pair)], v_ref[:, columns(pair)]
        end = s.end[pair]
        high, rest = split(diagonal(end))
        late = s.late[pair]
        d_key = s.d_key[pair] + late * nt(lanes(value, value), lanes(high, rest))
        d_value = s.d_value[pair] + late * nn(lanes(key, key), rows(high, rest))
        last_state = s.decay[0, pl.ds(pair, 1), :] * s.start[pair] + s.fresh[pair]
        ended = jnp.sum(last_state * end, axis=0, keepdims=True)
        change = s.query_part[pair] - d_key * key.astype(F32)
        change = change + jnp.where(last, ended, 0.0)
        mask = (head_of == 2 * pair + (side_of >= width).astype(jnp.int32)).astype(BF16)
        change_high, change_rest = split(change)
        per_head = nt(lanes(mask, mask), lanes(change_high, change_rest))
        return d_key, d_value, per_head

    def finish_pairs(index, carry):
        total = s.d_cum[...]
        results = [finish(index * UNROLL + offset) for offset in range(UNROLL)]
        for offset, (d_key, d_value, per_head) in enumerate(results):
            pair = index * UNROLL + offset
            dk_ref[:, columns(pair)] = d_key.astype(BF16)
            dv_ref[:, columns(pair)] = d_value.astype(BF16)
            total = total + per_head
        s.d_cum[...] = total
        return carry

    lax.fori_loop(0, pairs // UNROLL, finish_pairs, 0)
    dlog_ref[...] = nn(s.d_cum[...], causal.astype(F32), HIGH)


class Bag:
    pass


def layout(length, pairs, width, levels, chained, steps):
    pair_width = 2 * width
    state = (width, pair_width)
    token = (length, pair_width)
    wide = (length, 2 * length)
    dma = pltpu.SemaphoreType.DMA

    def vmem(shape, dtype=F32):
        return pltpu.VMEM(shape, dtype)

    spec = {
        "cum": vmem((2 * pairs, length)),
        "spread": vmem((2 * pairs, length, length)),
        "grow": vmem((pairs,) + token),
        "late": vmem((pairs,) + token),
        "decay": vmem((levels + 1, pairs, pair_width)),
        "decay_other": vmem((levels, pairs, pair_width)),
        "decay_send": dma((levels,)),
        "decay_recv": dma((levels,)),
        "fresh": vmem((pairs,) + state),
        "start": vmem((pairs,) + state),
        "incoming": vmem((pairs,) + state),
        "end": vmem((pairs,) + state),
        "table": vmem((pairs,) + wide),
        "score_high": vmem((pairs,) + wide, BF16),
        "score_rest": vmem((pairs,) + wide, BF16),
        "attended": vmem((pairs,) + token),
        "squares": vmem(token),
        "products": vmem(token),
        "inverse": vmem(token),
        "weight": vmem(token),
        "slope_high": vmem((pairs,) + token, BF16),
        "slope_rest": vmem((pairs,) + token, BF16),
        "gained": vmem((steps + 1, pairs, pair_width)),
        "gained_other": vmem((steps, pairs, pair_width)),
        "gain_send": dma((steps,)),
        "gain_recv": dma((steps,)),
        "query_part": vmem((pairs,) + token),
        "d_key": vmem((pairs,) + token),
        "d_value": vmem((pairs,) + token),
        "d_cum": vmem((2 * pairs, length)),
    }
    kept = [pairs >> (level + 1) for level in range(levels)]
    for name in ("forward", "backward"):
        for level in range(levels):
            for part in ("received", "first", "total", "give"):
                spec[name, part, level] = vmem((kept[level],) + state)
            if level > 0:
                spec[name, "prefix", level] = vmem((kept[level - 1],) + state)
        spec[name, "chain_in"] = vmem((chained,) + state)
        spec[name, "chain_out"] = vmem((chained,) + state)
        for part in ("chain_send", "chain_recv"):
            spec[name, part] = dma((chained,))
        for part in ("up_send", "up_recv", "down_send", "down_recv"):
            spec[name, part] = dma((levels,))
    return spec


def gathered(keys, refs):
    bag = Bag()
    bag.scans = {"forward": Bag(), "backward": Bag()}
    for key, ref in zip(keys, refs):
        if isinstance(key, str):
            setattr(bag, key, ref)
        elif len(key) == 2:
            setattr(bag.scans[key[0]], key[1], ref)
        else:
            scan = bag.scans[key[0]]
            if not hasattr(scan, key[1]):
                setattr(scan, key[1], {})
            getattr(scan, key[1])[key[2]] = ref
    return bag


def shards(size, queries, keys, values, log_decay, gain, d_out):
    seq_size, dp_size, levels = size
    length, features = queries.shape[1:]
    heads = log_decay.shape[1]
    width = features // heads
    pairs = heads // 2
    steps = (seq_size.bit_length() - 1) + (dp_size.bit_length() - 1)
    spec = layout(length, pairs, width, levels, pairs >> levels, steps)
    names = list(spec)

    def body(*refs):
        kernel(size, width, *refs[:11], gathered(names, refs[11:]))

    whole = pl.BlockSpec(memory_space=pltpu.VMEM)
    token = jax.ShapeDtypeStruct((length, features), BF16)
    flops = 2 * heads * length * width * (12 * length + 12 * width)
    d_queries, d_keys, d_values, d_log_decay, d_gain = pl.pallas_call(
        body,
        out_shape=(
            token, token, token,
            jax.ShapeDtypeStruct((heads, length), F32),
            jax.ShapeDtypeStruct((pairs, 2 * width), F32),
        ),
        in_specs=[whole] * 6,
        out_specs=(whole,) * 5,
        scratch_shapes=list(spec.values()),
        compiler_params=pltpu.CompilerParams(
            collective_id=0, has_side_effects=True, vmem_limit_bytes=48 * 1024 * 1024
        ),
        cost_estimate=pl.CostEstimate(
            flops=flops, bytes_accessed=14 * length * features, transcendentals=0
        ),
        name="gated_backward",
    )(queries[0], keys[0], values[0], log_decay[0], gain.reshape(pairs, 2 * width), d_out[0])
    return d_queries[None], d_keys[None], d_values[None], d_log_decay[None], d_gain.reshape(-1)


def solution(mesh):
    seq_size, dp_size = mesh.shape["seq"], mesh.shape["dp"]
    levels = seq_size.bit_length() // 2
    tokens = P("dp", "seq", None)
    decays = P("dp", None, "seq")
    return jax.shard_map(
        functools.partial(shards, (seq_size, dp_size, levels)),
        mesh=mesh,
        in_specs=(tokens, tokens, tokens, decays, P(), tokens),
        out_specs=(tokens, tokens, tokens, decays, P()),
        check_vma=False,
    )
```

```python
import functools

import jax
import jax.numpy as jnp
from jax import lax
from jax.experimental import pallas as pl
from jax.experimental.pallas import tpu as pltpu
from jax.sharding import PartitionSpec as P

EPSILON = 1e-06
HIGH = lax.Precision.HIGHEST
F32 = jnp.float32
BF16 = jnp.bfloat16
UNROLL = 2
VMEM = 58 * 1024 * 1024


def dot(a, b, contract, precision=None):
    return lax.dot_general(
        a, b, (contract, ((), ())), precision=precision, preferred_element_type=F32
    )


def nn(a, b, precision=None):
    return dot(a, b, ((1,), (0,)), precision)


def nt(a, b, precision=None):
    return dot(a, b, ((1,), (1,)), precision)


def tn(a, b):
    return dot(a, b, ((0,), (0,)))


def split(x):
    high = x.astype(BF16)
    return high, (x - high.astype(F32)).astype(BF16)


def rows(*parts):
    return jnp.concatenate(parts, axis=0)


def lanes(*parts):
    return jnp.concatenate(parts, axis=1)


def kernel(
    size,
    width,
    inputs,
    dq_ref, dk_ref, dv_ref, dlog_ref, dgain_ref,
    scratch,
):
    s = scratch
    q_ref, k_ref, v_ref, log_ref, gain_ref, do_ref = places = (
        s.q, s.k, s.v, s.log, s.gain, s.do
    )
    loads = [
        pltpu.make_async_copy(source, target, s.load.at[index])
        for index, (source, target) in enumerate(zip(inputs, places))
    ]
    q_load, k_load, v_load, log_load, gain_load, do_load = loads
    for load in (log_load, k_load, v_load, q_load, do_load, gain_load):
        load.start()
    seq_size, dp_size, levels = size
    length = q_ref.shape[0]
    pair_width = 2 * width
    pairs = q_ref.shape[1] // pair_width
    heads = 2 * pairs
    group = 2 ** levels
    chain = seq_size // group
    me = lax.axis_index("seq")
    dp = lax.axis_index("dp")

    def at_seq(index):
        return {"seq": index}

    def bit_of(value, level):
        return lax.rem(lax.div(value, 2 ** level), 2)

    def flipped(value, level):
        return value + 2 ** level * (1 - 2 * bit_of(value, level))

    place = lax.div(me, group)
    after = lax.rem(me + group, seq_size)
    before = lax.rem(me + seq_size - group, seq_size)
    seq_bits = seq_size.bit_length() - 1
    dp_bits = dp_size.bit_length() - 1
    partners = [at_seq(flipped(me, level)) for level in range(seq_bits)]
    partners += [{"dp": flipped(dp, level)} for level in range(dp_bits)]
    greeted = partners + [at_seq(after), at_seq(before)]

    barrier = pltpu.get_barrier_semaphore()
    for other in greeted:
        pl.semaphore_signal(
            barrier, inc=1, device_id=other, device_id_type=pl.DeviceIdType.MESH
        )

    def copy_to(source, target, send, recv, device):
        return pltpu.make_async_remote_copy(
            src_ref=source, dst_ref=target, send_sem=send, recv_sem=recv,
            device_id=device, device_id_type=pl.DeviceIdType.MESH,
        )

    lane_row = lax.broadcasted_iota(jnp.int32, (1, pair_width), 1)
    low_row = lane_row < width

    def low(shape):
        return lax.broadcasted_iota(jnp.int32, shape, 1) < width

    low_tok = low((length, pair_width))
    low_state = low((width, pair_width))

    def columns(pair):
        if isinstance(pair, int):
            return pl.ds(pair * pair_width, pair_width)
        return pl.ds(pl.multiple_of(pair * pair_width, pair_width), pair_width)

    def stacked(block):
        zero = jnp.zeros_like(block)
        return rows(jnp.where(low_tok, block, zero), jnp.where(low_tok, zero, block))

    def diagonal(state):
        zero = jnp.zeros_like(state)
        return rows(jnp.where(low_state, state, zero), jnp.where(low_state, zero, state))

    def packed(square):
        return jnp.where(low_state, square[:width], square[width:])

    upper_sub = lax.broadcasted_iota(jnp.int32, (pair_width, length), 0) < width

    def picked(broad):
        return jnp.where(upper_sub, broad[:, :length], broad[:, length:])

    def each(start, stop, compute, unroll=UNROLL):
        step = unroll if (stop - start) % unroll == 0 else 1

        def body(index, carry):
            stores = []
            for offset in range(step):
                stores += compute(start + index * step + offset)
            for ref, where, value in stores:
                ref[where] = value
            return carry

        lax.fori_loop(0, (stop - start) // step, body, 0)

    ones_from = lax.broadcasted_iota(jnp.int32, (length, length), 0)
    ones_to = lax.broadcasted_iota(jnp.int32, (length, length), 1)
    causal = ones_from >= ones_to
    log_load.wait()
    log_block = log_ref[...]
    cum_rows = nn(log_block, (ones_from <= ones_to).astype(F32), HIGH)
    s.cum[...] = cum_rows
    s.late_rows[...] = jnp.exp(cum_rows[:, length - 1:length] - cum_rows)
    cum_columns = nt(causal.astype(F32), log_block, HIGH)

    k_load.wait()
    v_load.wait()
    for pair in range(pairs):
        first = jnp.broadcast_to(cum_columns[:, 2 * pair:2 * pair + 1], (length, length))
        second = jnp.broadcast_to(cum_columns[:, 2 * pair + 1:2 * pair + 2], (length, length))
        s.spread[2 * pair] = first
        s.spread[2 * pair + 1] = second
        mixed = jnp.where(low_tok, first, second)
        total = mixed[length - 1:length, :]
        s.grow[pair] = jnp.exp(mixed)
        late = jnp.exp(total - mixed)
        s.late[pair] = late
        s.decay[0, pair:pair + 1, :] = jnp.exp(total)
        key = k_ref[:, columns(pair)]
        value = v_ref[:, columns(pair)].astype(F32) * late
        high, rest = split(value)
        key_t = jnp.transpose(key)
        s.key_t[pair] = key_t
        s.fresh[pair] = packed(nn(lanes(key_t, key_t), rows(high, rest)))

    pl.semaphore_wait(barrier, len(greeted))

    def scan(name, source, result, backward, works):
        x = s.scans[name]
        first_bit = 1 if backward else 0
        current, base, count = source, 0, pairs
        infos = []
        for level in range(levels):
            bit = bit_of(me, level)
            half = count // 2
            keep, give = bit * half, (1 - bit) * half
            partner = at_seq(flipped(me, level))
            copies = [
                copy_to(
                    current.at[pl.ds(give, half)], x.received[level],
                    x.up_send.at[level], x.up_recv.at[level], partner,
                )
            ]
            if not backward:
                copies.append(
                    copy_to(
                        s.decay.at[level], s.decay_other.at[level],
                        s.decay_send.at[level], s.decay_recv.at[level], partner,
                    )
                )
            for copy in copies:
                copy.start()
            works[level]()
            for copy in copies:
                copy.wait()
            if not backward:
                s.decay[level + 1] = s.decay[level] * s.decay_other[level]
            mine_first = jnp.broadcast_to(bit, (width, pair_width)) == first_bit
            mine_first_row = jnp.broadcast_to(bit, (1, pair_width)) == first_bit
            for i in range(half):
                own = current[keep + i]
                other = x.received[level][i]
                row = pl.ds(base + keep + i, 1)
                own_decay = s.decay[level, row, :]
                other_decay = s.decay_other[level, row, :]
                earlier = jnp.where(mine_first, own, other)
                later = jnp.where(mine_first, other, own)
                later_decay = jnp.where(mine_first_row, other_decay, own_decay)
                x.first[level][i] = earlier
                x.total[level][i] = later_decay * earlier + later
            infos.append((bit, half, keep, base, partner, mine_first, mine_first_row))
            current, base, count = x.total[level], base + keep, half

        start_place = chain - 1 if backward else 0
        stop_place = 0 if backward else chain - 1
        target = at_seq(before if backward else after)
        works[levels]()

        def link(i):
            return copy_to(
                x.chain_out.at[i], x.chain_in.at[i],
                x.chain_send.at[i], x.chain_recv.at[i], target,
            )

        @pl.when(place == start_place)
        def _():
            x.chain_in[...] = jnp.zeros_like(x.chain_in)

        for i in range(count):
            @pl.when(place != start_place)
            def _(i=i):
                link(i).wait_recv()

            @pl.when(place != stop_place)
            def _(i=i):
                row = pl.ds(base + i, 1)
                x.chain_out[i] = s.decay[levels, row, :] * x.chain_in[i] + current[i]
                link(i).start()

        prefix = x.chain_in
        for level in reversed(range(levels)):
            bit, half, keep, base, partner, mine_first, mine_first_row = infos[level]
            out = x.prefix[level] if level > 0 else result
            for i in range(half):
                row = pl.ds(base + keep + i, 1)
                own_decay = s.decay[level, row, :]
                other_decay = s.decay_other[level, row, :]
                first_decay = jnp.where(mine_first_row, own_decay, other_decay)
                given = prefix[i]
                moved = first_decay * given + x.first[level][i]
                x.give[level][i] = jnp.where(mine_first, moved, given)
                out[keep + i] = jnp.where(mine_first, given, moved)
            copy = copy_to(
                x.give[level], out.at[pl.ds(keep, half)],
                x.down_send.at[level], x.down_recv.at[level], partner,
            )
            copy.start()
            works[levels + 1 + levels - 1 - level]()
            copy.wait()
            prefix = out

        @pl.when(place != stop_place)
        def _():
            for i in range(count):
                link(i).wait_send()

    def inside(pair):
        query = q_ref[:, columns(pair)]
        scores = nt(query, stacked(k_ref[:, columns(pair)]))
        tables = []
        for head in range(2):
            gap = s.spread[2 * pair + head] - s.cum[pl.ds(2 * pair + head, 1), :]
            tables.append(jnp.where(causal, jnp.exp(jnp.minimum(gap, 0.0)), 0.0))
        table = lanes(*tables)
        high, rest = split(scores * table)
        values = stacked(v_ref[:, columns(pair)])
        part = nn(lanes(high, rest), rows(values, values))
        return [
            (s.table, pair, table), (s.score_high, pair, high),
            (s.score_rest, pair, rest), (s.attended, pair, part),
            (s.query_t, pair, jnp.transpose(query)),
        ]

    def nothing():
        pass

    def cut(shares, compute):
        works, start = [], 0
        for share in shares:
            stop = min(pairs, start + share)
            if stop > start:
                works.append(functools.partial(each, start, stop, compute))
            else:
                works.append(nothing)
            start = stop
        assert start == pairs
        return works

    def shares(near, far):
        counts = [near] + [far] * (levels - 1)
        return counts + [pairs - 2 * sum(counts)] + counts[::-1]

    even = shares(2, max(2, (pairs - 4 - 4) // max(1, 2 * (levels - 1)) // 2 * 2))
    q_load.wait()
    scan("forward", s.fresh, s.start, False, cut(even, inside))
    gain_load.wait()
    do_load.wait()

    s.squares[...] = jnp.zeros_like(s.squares)
    s.products[...] = jnp.zeros_like(s.products)

    def attend(pair):
        query = q_ref[:, columns(pair)]
        high, rest = split(diagonal(s.start[pair]))
        carried = nn(lanes(query, query), rows(high, rest))
        attended = s.attended[pair] + s.grow[pair] * carried
        slope = do_ref[:, columns(pair)].astype(F32) * gain_ref[pl.ds(pair, 1), :]
        return attended, slope

    def attend_pairs(index, carry):
        squares, products = s.squares[...], s.products[...]
        for offset in range(UNROLL):
            pair = index * UNROLL + offset
            attended, slope = attend(pair)
            s.attended[pair] = attended
            squares = squares + attended * attended
            products = products + attended * slope
        s.squares[...] = squares
        s.products[...] = products
        return carry

    lax.fori_loop(0, pairs // UNROLL, attend_pairs, 0)
    features = pairs * pair_width
    mean = jnp.sum(s.squares[...], axis=1, keepdims=True) / features
    inverse = 1.0 / jnp.sqrt(mean + EPSILON)
    weight = jnp.sum(s.products[...], axis=1, keepdims=True) / features * inverse * inverse * inverse
    s.inverse[...] = jnp.broadcast_to(inverse, (length, pair_width))
    s.weight[...] = jnp.broadcast_to(weight, (length, pair_width))

    def slopes(pair):
        cotangent = do_ref[:, columns(pair)].astype(F32)
        attended = s.attended[pair]
        inverse = s.inverse[...]
        gained = jnp.sum(attended * inverse * cotangent, axis=0, keepdims=True)
        slope = cotangent * gain_ref[pl.ds(pair, 1), :] * inverse - attended * s.weight[...]
        high, rest = split(slope)
        grown_high, grown_rest = split(slope * s.grow[pair])
        query_t = s.query_t[pair]
        incoming = packed(nn(lanes(query_t, query_t), rows(grown_high, grown_rest)))
        return [
            (s.slope_high, pair, high), (s.slope_rest, pair, rest),
            (s.incoming, pair, incoming),
            (s.gained, (0, pl.ds(pair, 1), slice(None)), gained),
        ]

    each(0, pairs, slopes)

    def gain_step(step):
        copy = copy_to(
            s.gained.at[step], s.gained_other.at[step],
            s.gain_send.at[step], s.gain_recv.at[step], partners[step],
        )
        return copy

    def gain_advance(step):
        gain_step(step).wait()
        s.gained[step + 1] = s.gained[step] + s.gained_other[step]
        if step + 1 < len(partners):
            gain_step(step + 1).start()

    gain_step(0).start()

    def grads(pair):
        query, key = q_ref[:, columns(pair)], k_ref[:, columns(pair)]
        keys, values = stacked(key), stacked(v_ref[:, columns(pair)])
        high, rest = s.slope_high[pair], s.slope_rest[pair]
        from_values = nt(lanes(high, rest), lanes(values, values))
        inner_high, inner_rest = split(from_values * s.table[pair])
        state_high, state_rest = split(diagonal(s.start[pair]))
        carried = nt(lanes(high, rest, high), lanes(state_high, state_high, state_rest))
        d_query = nn(lanes(inner_high, inner_rest), rows(keys, keys)) + s.grow[pair] * carried
        query_t = s.query_t[pair]
        d_key_t = picked(nn(lanes(query_t, query_t), rows(inner_high, inner_rest)))
        score_high, score_rest = s.score_high[pair], s.score_rest[pair]
        high_t, rest_t = jnp.transpose(high), jnp.transpose(rest)
        d_value_t = picked(
            nn(lanes(high_t, high_t, rest_t), rows(score_high, score_rest, score_high))
        )
        change_high, change_rest = split(d_query * query.astype(F32))
        per_head = nt(lanes(sides, sides), lanes(change_high, change_rest))
        return [
            (dq_ref, (slice(None), columns(pair)), d_query.astype(BF16)),
            (s.query_rows, pair, per_head),
            (s.d_key_t, pair, d_key_t), (s.d_value, pair, jnp.transpose(d_value_t)),
        ]

    side_row = lax.broadcasted_iota(jnp.int32, (8, pair_width), 0)
    side_lane = lax.broadcasted_iota(jnp.int32, (8, pair_width), 1)
    sides = (side_row == (side_lane >= width).astype(jnp.int32)).astype(F32).astype(BF16)
    works = cut(even, grads)
    steps = len(partners)
    pieces = [(steps * i // len(works), steps * (i + 1) // len(works)) for i in range(len(works))]

    def with_gain(work, piece):
        def run():
            work()
            for step in range(*piece):
                gain_advance(step)
        return run

    scan("backward", s.incoming, s.end, True, [with_gain(*both) for both in zip(works, pieces)])
    dgain_ref[...] = s.gained[steps]

    s.d_cum[...] = jnp.zeros_like(s.d_cum)
    s.ended[...] = jnp.zeros_like(s.ended)
    head_of = lax.broadcasted_iota(jnp.int32, (heads, pair_width), 0)
    side_of = (lax.broadcasted_iota(jnp.int32, (heads, pair_width), 1) >= width).astype(jnp.int32)

    def finish(pair):
        key, value = k_ref[:, columns(pair)], v_ref[:, columns(pair)]
        end = s.end[pair]
        high, rest = split(diagonal(end))
        late_t = jnp.where(
            upper_sub, s.late_rows[pl.ds(2 * pair, 1), :], s.late_rows[pl.ds(2 * pair + 1, 1), :]
        )
        d_key_t = s.d_key_t[pair] + late_t * nt(lanes(high, rest), lanes(value, value))
        d_value = s.d_value[pair] + s.late[pair] * nn(lanes(key, key), rows(high, rest))
        change = d_key_t * s.key_t[pair].astype(F32)
        first = s.query_rows[pair, 0:1] - jnp.sum(change[:width], axis=0, keepdims=True)
        second = s.query_rows[pair, 1:2] - jnp.sum(change[width:], axis=0, keepdims=True)
        d_cum = jnp.where(head_of == 2 * pair, first, 0.0)
        d_cum = jnp.where(head_of == 2 * pair + 1, second, d_cum)
        last_state = s.decay[0, pl.ds(pair, 1), :] * s.start[pair] + s.fresh[pair]
        ended = jnp.sum(last_state * end, axis=0, keepdims=True)
        ended = jnp.where(head_of == 2 * pair + side_of, ended, 0.0)
        return jnp.transpose(d_key_t.astype(BF16)), d_value.astype(BF16), d_cum, ended

    def finish_pairs(index, carry):
        total, ends = s.d_cum[...], s.ended[...]
        results = [finish(index * UNROLL + offset) for offset in range(UNROLL)]
        for offset, (d_key, d_value, d_cum, ended) in enumerate(results):
            pair = index * UNROLL + offset
            dk_ref[:, columns(pair)] = d_key
            dv_ref[:, columns(pair)] = d_value
            total = total + d_cum
            ends = ends + ended
        s.d_cum[...] = total
        s.ended[...] = ends
        return carry

    lax.fori_loop(0, pairs // UNROLL, finish_pairs, 0)
    through = jnp.sum(s.ended[...], axis=1, keepdims=True)
    dlog_ref[...] = nn(s.d_cum[...], causal.astype(F32), HIGH) + through


def deliver(*refs):
    sources, targets, done = refs[:5], refs[5:10], refs[10]
    copies = [
        pltpu.make_async_copy(source, target, done.at[index])
        for index, (source, target) in enumerate(zip(sources, targets))
    ]
    for copy in copies:
        copy.start()
    for copy in copies:
        copy.wait()


class Bag:
    pass


def layout(length, pairs, width, levels, chained, steps):
    pair_width = 2 * width
    state = (width, pair_width)
    token = (length, pair_width)
    wide = (length, 2 * length)
    dma = pltpu.SemaphoreType.DMA

    def vmem(shape, dtype=F32):
        return pltpu.VMEM(shape, dtype)

    spec = {
        "cum": vmem((2 * pairs, length)),
        "spread": vmem((2 * pairs, length, length)),
        "grow": vmem((pairs,) + token),
        "late": vmem((pairs,) + token),
        "decay": vmem((levels + 1, pairs, pair_width)),
        "decay_other": vmem((levels, pairs, pair_width)),
        "decay_send": dma((levels,)),
        "decay_recv": dma((levels,)),
        "fresh": vmem((pairs,) + state),
        "start": vmem((pairs,) + state),
        "incoming": vmem((pairs,) + state),
        "end": vmem((pairs,) + state),
        "table": vmem((pairs,) + wide),
        "score_high": vmem((pairs,) + wide, BF16),
        "score_rest": vmem((pairs,) + wide, BF16),
        "attended": vmem((pairs,) + token),
        "squares": vmem(token),
        "products": vmem(token),
        "inverse": vmem(token),
        "weight": vmem(token),
        "slope_high": vmem((pairs,) + token, BF16),
        "slope_rest": vmem((pairs,) + token, BF16),
        "gained": vmem((steps + 1, pairs, pair_width)),
        "gained_other": vmem((steps, pairs, pair_width)),
        "gain_send": dma((steps,)),
        "gain_recv": dma((steps,)),
        "query_rows": vmem((pairs, 8, length)),
        "query_t": vmem((pairs, pair_width, length), BF16),
        "key_t": vmem((pairs, pair_width, length), BF16),
        "late_rows": vmem((2 * pairs, length)),
        "d_key_t": vmem((pairs, pair_width, length)),
        "ended": vmem((2 * pairs, pair_width)),
        "q": vmem((length, pairs * pair_width), BF16),
        "k": vmem((length, pairs * pair_width), BF16),
        "v": vmem((length, pairs * pair_width), BF16),
        "do": vmem((length, pairs * pair_width), BF16),
        "log": vmem((2 * pairs, length)),
        "gain": vmem((pairs, pair_width)),
        "load": dma((6,)),
        "d_value": vmem((pairs,) + token),
        "d_cum": vmem((2 * pairs, length)),
    }
    kept = [pairs >> (level + 1) for level in range(levels)]
    for name in ("forward", "backward"):
        for level in range(levels):
            for part in ("received", "first", "total", "give"):
                spec[name, part, level] = vmem((kept[level],) + state)
            if level > 0:
                spec[name, "prefix", level] = vmem((kept[level - 1],) + state)
        spec[name, "chain_in"] = vmem((chained,) + state)
        spec[name, "chain_out"] = vmem((chained,) + state)
        for part in ("chain_send", "chain_recv"):
            spec[name, part] = dma((chained,))
        for part in ("up_send", "up_recv", "down_send", "down_recv"):
            spec[name, part] = dma((levels,))
    return spec


def gathered(keys, refs):
    bag = Bag()
    bag.scans = {"forward": Bag(), "backward": Bag()}
    for key, ref in zip(keys, refs):
        if isinstance(key, str):
            setattr(bag, key, ref)
        elif len(key) == 2:
            setattr(bag.scans[key[0]], key[1], ref)
        else:
            scan = bag.scans[key[0]]
            if not hasattr(scan, key[1]):
                setattr(scan, key[1], {})
            getattr(scan, key[1])[key[2]] = ref
    return bag


def shards(size, queries, keys, values, log_decay, gain, d_out):
    seq_size, dp_size, levels = size
    length, features = queries.shape[1:]
    heads = log_decay.shape[1]
    width = features // heads
    pairs = heads // 2
    steps = (seq_size.bit_length() - 1) + (dp_size.bit_length() - 1)
    spec = layout(length, pairs, width, levels, pairs >> levels, steps)
    names = list(spec)

    def body(*refs):
        kernel(size, width, refs[:6], *refs[6:11], gathered(names, refs[11:]))

    whole = pl.BlockSpec(memory_space=pltpu.VMEM)
    token = jax.ShapeDtypeStruct((length, features), BF16)
    flops = 2 * heads * length * width * (12 * length + 12 * width)
    results = (
        token, token, token,
        jax.ShapeDtypeStruct((heads, length), F32),
        jax.ShapeDtypeStruct((pairs, 2 * width), F32),
    )
    outputs = pl.pallas_call(
        body,
        out_shape=results,
        in_specs=[pl.BlockSpec(memory_space=pltpu.HBM)] * 6,
        out_specs=(whole,) * 5,
        scratch_shapes=list(spec.values()),
        compiler_params=pltpu.CompilerParams(
            collective_id=0, has_side_effects=True, vmem_limit_bytes=VMEM
        ),
        cost_estimate=pl.CostEstimate(
            flops=flops, bytes_accessed=14 * length * features, transcendentals=0
        ),
        name="gated_backward",
    )(queries[0], keys[0], values[0], log_decay[0], gain.reshape(pairs, 2 * width), d_out[0])
    d_queries, d_keys, d_values, d_log_decay, d_gain = pl.pallas_call(
        deliver,
        out_shape=results,
        in_specs=[pl.BlockSpec(memory_space=pl.ANY)] * 5,
        out_specs=(pl.BlockSpec(memory_space=pltpu.HBM),) * 5,
        scratch_shapes=[pltpu.SemaphoreType.DMA((5,))],
        compiler_params=pltpu.CompilerParams(vmem_limit_bytes=VMEM),
        cost_estimate=pl.CostEstimate(
            flops=0, bytes_accessed=12 * length * features, transcendentals=0
        ),
        name="deliver",
    )(*outputs)
    return d_queries[None], d_keys[None], d_values[None], d_log_decay[None], d_gain.reshape(-1)


def solution(mesh):
    seq_size, dp_size = mesh.shape["seq"], mesh.shape["dp"]
    levels = seq_size.bit_length() // 2
    tokens = P("dp", "seq", None)
    decays = P("dp", None, "seq")
    return jax.shard_map(
        functools.partial(shards, (seq_size, dp_size, levels)),
        mesh=mesh,
        in_specs=(tokens, tokens, tokens, decays, P(), tokens),
        out_specs=(tokens, tokens, tokens, decays, P()),
        check_vma=False,
    )
```

```python
import functools

import jax
import jax.numpy as jnp
from jax import lax
from jax.experimental import pallas as pl
from jax.experimental.pallas import tpu as pltpu
from jax.sharding import PartitionSpec as P

EPSILON = 1e-06
HIGH = lax.Precision.HIGHEST
F32 = jnp.float32
BF16 = jnp.bfloat16
UNROLL = 2
WIDE = 4
VMEM = 58 * 1024 * 1024


def dot(a, b, contract, precision=None):
    return lax.dot_general(
        a, b, (contract, ((), ())), precision=precision, preferred_element_type=F32
    )


def nn(a, b, precision=None):
    return dot(a, b, ((1,), (0,)), precision)


def nt(a, b, precision=None):
    return dot(a, b, ((1,), (1,)), precision)


def tn(a, b):
    return dot(a, b, ((0,), (0,)))


def split(x):
    high = x.astype(BF16)
    return high, (x - high.astype(F32)).astype(BF16)


def rows(*parts):
    return jnp.concatenate(parts, axis=0)


def lanes(*parts):
    return jnp.concatenate(parts, axis=1)


def kernel(
    size,
    width,
    inputs,
    outputs,
    scratch,
):
    s = scratch
    dq_ref, dk_ref, dv_ref, dlog_ref, dgain_ref = s.dq, s.dk, s.dv, s.dlog, s.dgain
    q_ref, k_ref, v_ref, log_ref, gain_ref, do_ref = places = (
        s.q, s.k, s.v, s.log, s.gain, s.do
    )
    loads = [
        pltpu.make_async_copy(source, target, s.load.at[index])
        for index, (source, target) in enumerate(zip(inputs, places))
    ]
    q_load, k_load, v_load, log_load, gain_load, do_load = loads
    for load in (log_load, k_load, v_load, q_load, do_load, gain_load):
        load.start()
    seq_size, dp_size, levels = size
    length = q_ref.shape[0]
    pair_width = 2 * width
    pairs = q_ref.shape[1] // pair_width
    heads = 2 * pairs
    group = 2 ** levels
    chain = seq_size // group
    me = lax.axis_index("seq")
    dp = lax.axis_index("dp")

    def at_seq(index):
        return {"seq": index}

    def bit_of(value, level):
        return lax.rem(lax.div(value, 2 ** level), 2)

    def flipped(value, level):
        return value + 2 ** level * (1 - 2 * bit_of(value, level))

    place = lax.div(me, group)
    after = lax.rem(me + group, seq_size)
    before = lax.rem(me + seq_size - group, seq_size)
    seq_bits = seq_size.bit_length() - 1
    dp_bits = dp_size.bit_length() - 1
    partners = [at_seq(flipped(me, level)) for level in range(seq_bits)]
    partners += [{"dp": flipped(dp, level)} for level in range(dp_bits)]
    greeted = partners + [at_seq(after), at_seq(before)]

    barrier = pltpu.get_barrier_semaphore()
    for other in greeted:
        pl.semaphore_signal(
            barrier, inc=1, device_id=other, device_id_type=pl.DeviceIdType.MESH
        )

    def copy_to(source, target, send, recv, device):
        return pltpu.make_async_remote_copy(
            src_ref=source, dst_ref=target, send_sem=send, recv_sem=recv,
            device_id=device, device_id_type=pl.DeviceIdType.MESH,
        )

    lane_row = lax.broadcasted_iota(jnp.int32, (1, pair_width), 1)
    low_row = lane_row < width

    def low(shape):
        return lax.broadcasted_iota(jnp.int32, shape, 1) < width

    low_tok = low((length, pair_width))
    low_state = low((width, pair_width))

    def columns(pair):
        if isinstance(pair, int):
            return pl.ds(pair * pair_width, pair_width)
        return pl.ds(pl.multiple_of(pair * pair_width, pair_width), pair_width)

    def stacked(block):
        zero = jnp.zeros_like(block)
        return rows(jnp.where(low_tok, block, zero), jnp.where(low_tok, zero, block))

    def diagonal(state):
        zero = jnp.zeros_like(state)
        return rows(jnp.where(low_state, state, zero), jnp.where(low_state, zero, state))

    def packed(square):
        return jnp.where(low_state, square[:width], square[width:])

    upper_sub = lax.broadcasted_iota(jnp.int32, (pair_width, length), 0) < width

    def picked(broad):
        return jnp.where(upper_sub, broad[:, :length], broad[:, length:])

    def each(start, count, compute, unroll=UNROLL):
        if isinstance(count, int) and count % unroll:
            unroll = 1

        def body(index, carry):
            stores = []
            for offset in range(unroll):
                stores += compute(start + index * unroll + offset)
            for ref, where, value in stores:
                ref[where] = value
            return carry

        trips = count // unroll if isinstance(count, int) else lax.div(count, unroll)
        lax.fori_loop(0, trips, body, 0)

    ones_from = lax.broadcasted_iota(jnp.int32, (length, length), 0)
    ones_to = lax.broadcasted_iota(jnp.int32, (length, length), 1)
    causal = ones_from >= ones_to
    log_load.wait()
    log_block = log_ref[...]
    cum_rows = nn(log_block, (ones_from <= ones_to).astype(F32), HIGH)
    s.cum[...] = cum_rows
    s.late_rows[...] = jnp.exp(cum_rows[:, length - 1:length] - cum_rows)
    cum_columns = nt(causal.astype(F32), log_block, HIGH)

    k_load.wait()
    v_load.wait()
    for pair in range(pairs):
        first = jnp.broadcast_to(cum_columns[:, 2 * pair:2 * pair + 1], (length, length))
        second = jnp.broadcast_to(cum_columns[:, 2 * pair + 1:2 * pair + 2], (length, length))
        s.spread[2 * pair] = first
        s.spread[2 * pair + 1] = second
        mixed = jnp.where(low_tok, first, second)
        total = mixed[length - 1:length, :]
        s.grow[pair] = jnp.exp(mixed)
        late = jnp.exp(total - mixed)
        s.late[pair] = late
        s.decay[0, pair:pair + 1, :] = jnp.exp(total)

    def state_of(pair):
        key = k_ref[:, columns(pair)]
        high, rest = split(v_ref[:, columns(pair)].astype(F32) * s.late[pair])
        key_t = jnp.transpose(key)
        fresh = packed(nn(lanes(key_t, key_t), rows(high, rest)))
        return [(s.key_t, pair, key_t), (s.fresh, pair, fresh)]

    pl.semaphore_wait(barrier, len(greeted))

    bits = [bit_of(me, level) for level in range(levels)]
    halves = [pairs >> (level + 1) for level in range(levels)]
    keeps = [bit * half for bit, half in zip(bits, halves)]
    gives = [(1 - bit) * half for bit, half in zip(bits, halves)]
    bases = [0]
    for keep in keeps:
        bases.append(bases[-1] + keep)
    state_shape = (width, pair_width)

    def pieces(level):
        half = halves[level]
        if level == levels - 1:
            return [(i, 1) for i in range(half)]
        return [(gives[level + 1], half // 2), (keeps[level + 1], half // 2)]

    def scan(name, source, result, backward, produce, works, consume):
        x = s.scans[name]
        first_bit = 1 if backward else 0
        owned = [source] + [x.total[level] for level in range(levels)]
        outs = [result] + [x.prefix[level] for level in range(1, levels)]
        mine_first = [jnp.broadcast_to(bit, state_shape) == first_bit for bit in bits]
        row_first = [jnp.broadcast_to(bit, (1, pair_width)) == first_bit for bit in bits]
        partner = [at_seq(flipped(me, level)) for level in range(levels)]

        def up(level, index):
            offset, size = pieces(level)[index]
            return copy_to(
                owned[level].at[pl.ds(gives[level] + offset, size)],
                x.received[level].at[pl.ds(offset, size)],
                x.up_send.at[level, index], x.up_recv.at[level, index], partner[level],
            )

        def decay_copy(level):
            return copy_to(
                s.decay.at[level], s.decay_other.at[level],
                s.decay_send.at[level], s.decay_recv.at[level], partner[level],
            )

        def start_up(level):
            if not backward:
                decay_copy(level).start()
            for index in range(len(pieces(level))):
                up(level, index).start()

        def join(level, index):
            up(level, index).wait_recv()
            offset, size = pieces(level)[index]
            for i in range(size):
                own = owned[level][keeps[level] + offset + i]
                other = x.received[level][offset + i]
                row = pl.ds(bases[level] + keeps[level] + offset + i, 1)
                later_decay = jnp.where(
                    row_first[level], s.decay_other[level, row, :], s.decay[level, row, :]
                )
                earlier = jnp.where(mine_first[level], own, other)
                later = jnp.where(mine_first[level], other, own)
                x.first[level][offset + i] = earlier
                x.total[level][offset + i] = later_decay * earlier + later

        produce(gives[0], halves[0])
        start_up(0)
        produce(keeps[0], halves[0])
        for level in range(levels):
            works[level]()
            if not backward:
                decay_copy(level).wait()
                s.decay[level + 1] = s.decay[level] * s.decay_other[level]
            if level < levels - 1:
                join(level, 0)
                start_up(level + 1)
                join(level, 1)

        start_place = chain - 1 if backward else 0
        stop_place = 0 if backward else chain - 1
        target = at_seq(before if backward else after)
        count = halves[-1]

        def link(i):
            return copy_to(
                x.chain_out.at[i], x.chain_in.at[i],
                x.chain_send.at[i], x.chain_recv.at[i], target,
            )

        def down(level, i):
            place_of = keeps[level] + i
            return copy_to(
                x.give[level].at[i], outs[level].at[place_of],
                x.down_send.at[level, i], x.down_recv.at[level, i], partner[level],
            )

        def arrival(level, i):
            return copy_to(
                x.give[level].at[i], outs[level].at[gives[level] + i],
                x.down_send.at[level, i], x.down_recv.at[level, i], partner[level],
            )

        def descend(level, i, given):
            row = pl.ds(bases[level] + keeps[level] + i, 1)
            first_decay = jnp.where(
                row_first[level], s.decay[level, row, :], s.decay_other[level, row, :]
            )
            moved = first_decay * given + x.first[level][i]
            x.give[level][i] = jnp.where(mine_first[level], moved, given)
            down(level, i).start()
            own = jnp.where(mine_first[level], given, moved)
            outs[level][keeps[level] + i] = own
            if level > 0:
                descend(level - 1, keeps[level] + i, own)

        @pl.when(place == start_place)
        def _():
            x.chain_in[...] = jnp.zeros_like(x.chain_in)

        begins = (place == start_place).astype(jnp.int32)
        for i in range(count):
            join(levels - 1, i)
        works[levels](1 - begins)
        for i in range(count):
            @pl.when(place != start_place)
            def _(i=i):
                link(i).wait_recv()

            @pl.when(place != stop_place)
            def _(i=i):
                row = pl.ds(bases[levels] + i, 1)
                x.chain_out[i] = s.decay[levels, row, :] * x.chain_in[i] + owned[levels][i]
                link(i).start()

            descend(levels - 1, i, x.chain_in[i])
        works[levels + 1](begins)
        for level in range(levels - 1, 0, -1):
            order = range(halves[level])
            for i in order if level == levels - 1 else ordered(level):
                arrival(level, i).wait_recv()
                descend(level - 1, gives[level] + i, outs[level][gives[level] + i])
        consume(keeps[0], halves[0])
        for i in range(halves[0]):
            arrival(0, i).wait_recv()
        consume(gives[0], halves[0])

        for level in range(levels):
            for index in range(len(pieces(level))):
                up(level, index).wait_send()
            for i in range(halves[level]):
                down(level, i).wait_send()

        @pl.when(place != stop_place)
        def _():
            for i in range(count):
                link(i).wait_send()

    def ordered(level):
        half = halves[level + 1]
        return [keeps[level + 1] + i for i in range(half)] + [
            gives[level + 1] + i for i in range(half)
        ]

    def inside(pair):
        query = q_ref[:, columns(pair)]
        scores = nt(query, stacked(k_ref[:, columns(pair)]))
        tables = []
        for head in range(2):
            gap = s.spread[2 * pair + head] - s.cum[pl.ds(2 * pair + head, 1), :]
            tables.append(jnp.where(causal, jnp.exp(jnp.minimum(gap, 0.0)), 0.0))
        table = lanes(*tables)
        high, rest = split(scores * table)
        values = stacked(v_ref[:, columns(pair)])
        part = nn(lanes(high, rest), rows(values, values))
        return [
            (s.table, pair, table), (s.score_high, pair, high),
            (s.score_rest, pair, rest), (s.attended, pair, part),
            (s.query_t, pair, jnp.transpose(query)),
        ]

    def cut(compute):
        share = max(2, pairs // (2 * levels) // 2 * 2)
        counts = [2] + [share] * (levels - 1)
        left = pairs - sum(counts)
        middle = left // 2 // 2 * 2
        works, start = [], 0
        for count in counts:
            works.append(functools.partial(each, start, count, compute))
            start += count

        def waiting(flag):
            each(start, middle * flag, compute)

        def closing(flag):
            done = middle * (1 - flag)
            each(start + done, left - done, compute)

        return works + [waiting, closing]

    s.squares[...] = jnp.zeros_like(s.squares)
    s.products[...] = jnp.zeros_like(s.products)

    def attend(pair):
        query = q_ref[:, columns(pair)]
        high, rest = split(diagonal(s.start[pair]))
        carried = nn(lanes(query, query), rows(high, rest))
        attended = s.attended[pair] + s.grow[pair] * carried
        slope = do_ref[:, columns(pair)].astype(F32) * gain_ref[pl.ds(pair, 1), :]
        return attended, slope

    def attend_range(start, count):
        def body(index, carry):
            squares, products = s.squares[...], s.products[...]
            results = [attend(start + index * WIDE + offset) for offset in range(WIDE)]
            for offset, (attended, slope) in enumerate(results):
                s.attended[start + index * WIDE + offset] = attended
                squares = squares + attended * attended
                products = products + attended * slope
            s.squares[...] = squares
            s.products[...] = products
            return carry

        lax.fori_loop(0, count // WIDE, body, 0)

    q_load.wait()
    arrived = []

    def attend_after_loads(start, count):
        if not arrived:
            gain_load.wait()
            do_load.wait()
            arrived.append(True)
        attend_range(start, count)

    scan(
        "forward", s.fresh, s.start, False,
        lambda start, count: each(start, count, state_of, WIDE),
        cut(inside), attend_after_loads,
    )
    features = pairs * pair_width
    mean = jnp.sum(s.squares[...], axis=1, keepdims=True) / features
    inverse = 1.0 / jnp.sqrt(mean + EPSILON)
    weight = jnp.sum(s.products[...], axis=1, keepdims=True) / features * inverse * inverse * inverse
    s.inverse[...] = jnp.broadcast_to(inverse, (length, pair_width))
    s.weight[...] = jnp.broadcast_to(weight, (length, pair_width))

    def slopes(pair):
        cotangent = do_ref[:, columns(pair)].astype(F32)
        attended = s.attended[pair]
        inverse = s.inverse[...]
        gained = jnp.sum(attended * inverse * cotangent, axis=0, keepdims=True)
        slope = cotangent * gain_ref[pl.ds(pair, 1), :] * inverse - attended * s.weight[...]
        high, rest = split(slope)
        grown_high, grown_rest = split(slope * s.grow[pair])
        query_t = s.query_t[pair]
        incoming = packed(nn(lanes(query_t, query_t), rows(grown_high, grown_rest)))
        return [
            (s.slope_high, pair, high), (s.slope_rest, pair, rest),
            (s.incoming, pair, incoming),
            (s.gained, (0, pl.ds(pair, 1), slice(None)), gained),
        ]

    def gain_step(step):
        copy = copy_to(
            s.gained.at[step], s.gained_other.at[step],
            s.gain_send.at[step], s.gain_recv.at[step], partners[step],
        )
        return copy

    def gain_advance(step):
        gain_step(step).wait()
        s.gained[step + 1] = s.gained[step] + s.gained_other[step]
        if step + 1 < len(partners):
            gain_step(step + 1).start()

    def grads(pair):
        query, key = q_ref[:, columns(pair)], k_ref[:, columns(pair)]
        keys, values = stacked(key), stacked(v_ref[:, columns(pair)])
        high, rest = s.slope_high[pair], s.slope_rest[pair]
        from_values = nt(lanes(high, rest), lanes(values, values))
        inner_high, inner_rest = split(from_values * s.table[pair])
        state_high, state_rest = split(diagonal(s.start[pair]))
        carried = nt(lanes(high, rest, high), lanes(state_high, state_high, state_rest))
        d_query = nn(lanes(inner_high, inner_rest), rows(keys, keys)) + s.grow[pair] * carried
        query_t = s.query_t[pair]
        d_key_t = picked(nn(lanes(query_t, query_t), rows(inner_high, inner_rest)))
        score_high, score_rest = s.score_high[pair], s.score_rest[pair]
        high_t, rest_t = jnp.transpose(high), jnp.transpose(rest)
        d_value_t = picked(
            nn(lanes(high_t, high_t, rest_t), rows(score_high, score_rest, score_high))
        )
        change_high, change_rest = split(d_query * query.astype(F32))
        per_head = nt(lanes(sides, sides), lanes(change_high, change_rest))
        return [
            (dq_ref, (slice(None), columns(pair)), d_query.astype(BF16)),
            (s.query_rows, pair, per_head),
            (s.d_key_t, pair, d_key_t), (s.d_value, pair, jnp.transpose(d_value_t)),
        ]

    side_row = lax.broadcasted_iota(jnp.int32, (8, pair_width), 0)
    side_lane = lax.broadcasted_iota(jnp.int32, (8, pair_width), 1)
    sides = (side_row == (side_lane >= width).astype(jnp.int32)).astype(F32).astype(BF16)
    steps = len(partners)

    def with_gain(work, first, last):
        def run(*flag):
            work(*flag)
            for step in range(first, last):
                gain_advance(step)
        return run

    works = cut(grads)
    begun = []

    def produce_slopes(start, count):
        each(start, count, slopes, WIDE)
        begun.append(True)
        if len(begun) == 2:
            gain_step(0).start()

    spread_steps = [steps * i // (levels + 2) for i in range(levels + 3)]
    works = [
        with_gain(work, spread_steps[i], spread_steps[i + 1]) for i, work in enumerate(works)
    ]

    def store(index):
        return pltpu.make_async_copy(results[index], outputs[index], s.store.at[index, 0])

    results = (dq_ref, dk_ref, dv_ref, dlog_ref, dgain_ref)
    stores = []

    s.d_cum[...] = jnp.zeros_like(s.d_cum)
    s.ended[...] = jnp.zeros_like(s.ended)
    head_of = lax.broadcasted_iota(jnp.int32, (heads, pair_width), 0)
    side_of = (lax.broadcasted_iota(jnp.int32, (heads, pair_width), 1) >= width).astype(jnp.int32)

    def finish(pair):
        key, value = k_ref[:, columns(pair)], v_ref[:, columns(pair)]
        end = s.end[pair]
        high, rest = split(diagonal(end))
        late_t = jnp.where(
            upper_sub, s.late_rows[pl.ds(2 * pair, 1), :], s.late_rows[pl.ds(2 * pair + 1, 1), :]
        )
        d_key_t = s.d_key_t[pair] + late_t * nt(lanes(high, rest), lanes(value, value))
        d_value = s.d_value[pair] + s.late[pair] * nn(lanes(key, key), rows(high, rest))
        change = d_key_t * s.key_t[pair].astype(F32)
        first = s.query_rows[pair, 0:1] - jnp.sum(change[:width], axis=0, keepdims=True)
        second = s.query_rows[pair, 1:2] - jnp.sum(change[width:], axis=0, keepdims=True)
        d_cum = jnp.where(head_of == 2 * pair, first, 0.0)
        d_cum = jnp.where(head_of == 2 * pair + 1, second, d_cum)
        last_state = s.decay[0, pl.ds(pair, 1), :] * s.start[pair] + s.fresh[pair]
        ended = jnp.sum(last_state * end, axis=0, keepdims=True)
        ended = jnp.where(head_of == 2 * pair + side_of, ended, 0.0)
        return jnp.transpose(d_key_t.astype(BF16)), d_value.astype(BF16), d_cum, ended

    def finish_range(start, count):
        if not stores:
            dgain_ref[...] = s.gained[steps]
            begin = [store(0), store(4)]
            for copy in begin:
                copy.start()
            stores.extend(begin)

        def body(index, carry):
            total, ends = s.d_cum[...], s.ended[...]
            results = [finish(start + index * WIDE + offset) for offset in range(WIDE)]
            for offset, (d_key, d_value, d_cum, ended) in enumerate(results):
                pair = start + index * WIDE + offset
                dk_ref[:, columns(pair)] = d_key
                dv_ref[:, columns(pair)] = d_value
                total = total + d_cum
                ends = ends + ended
            s.d_cum[...] = total
            s.ended[...] = ends
            return carry

        lax.fori_loop(0, count // WIDE, body, 0)
        where = pl.ds(pl.multiple_of(start * pair_width, pair_width), count * pair_width)
        slot = len(stores) // 4
        for index in (1, 2):
            copy = pltpu.make_async_copy(
                results[index].at[:, where], outputs[index].at[:, where], s.store.at[index, slot]
            )
            copy.start()
            stores.append(copy)

    scan("backward", s.incoming, s.end, True, produce_slopes, works, finish_range)
    through = jnp.sum(s.ended[...], axis=1, keepdims=True)
    dlog_ref[...] = nn(s.d_cum[...], causal.astype(F32), HIGH) + through
    stores.append(store(3))
    stores[-1].start()
    for copy in stores:
        copy.wait()


def deliver(*refs):
    sources, targets, held, (read, wrote) = refs[:5], refs[5:10], refs[10:15], refs[15:]
    reads = [
        pltpu.make_async_copy(source, place, read.at[index])
        for index, (source, place) in enumerate(zip(sources, held))
    ]
    writes = [
        pltpu.make_async_copy(place, target, wrote.at[index])
        for index, (place, target) in enumerate(zip(held, targets))
    ]
    for copy in reads:
        copy.start()
    for copy, following in zip(reads, writes):
        copy.wait()
        following.start()
    for copy in writes:
        copy.wait()


class Bag:
    pass


def layout(length, pairs, width, levels, chained, steps):
    pair_width = 2 * width
    state = (width, pair_width)
    token = (length, pair_width)
    wide = (length, 2 * length)
    dma = pltpu.SemaphoreType.DMA

    def vmem(shape, dtype=F32):
        return pltpu.VMEM(shape, dtype)

    spec = {
        "cum": vmem((2 * pairs, length)),
        "spread": vmem((2 * pairs, length, length)),
        "grow": vmem((pairs,) + token),
        "late": vmem((pairs,) + token),
        "decay": vmem((levels + 1, pairs, pair_width)),
        "decay_other": vmem((levels, pairs, pair_width)),
        "decay_send": dma((levels,)),
        "decay_recv": dma((levels,)),
        "fresh": vmem((pairs,) + state),
        "start": vmem((pairs,) + state),
        "incoming": vmem((pairs,) + state),
        "end": vmem((pairs,) + state),
        "table": vmem((pairs,) + wide),
        "score_high": vmem((pairs,) + wide, BF16),
        "score_rest": vmem((pairs,) + wide, BF16),
        "attended": vmem((pairs,) + token),
        "squares": vmem(token),
        "products": vmem(token),
        "inverse": vmem(token),
        "weight": vmem(token),
        "slope_high": vmem((pairs,) + token, BF16),
        "slope_rest": vmem((pairs,) + token, BF16),
        "gained": vmem((steps + 1, pairs, pair_width)),
        "gained_other": vmem((steps, pairs, pair_width)),
        "gain_send": dma((steps,)),
        "gain_recv": dma((steps,)),
        "query_rows": vmem((pairs, 8, length)),
        "query_t": vmem((pairs, pair_width, length), BF16),
        "key_t": vmem((pairs, pair_width, length), BF16),
        "late_rows": vmem((2 * pairs, length)),
        "d_key_t": vmem((pairs, pair_width, length)),
        "ended": vmem((2 * pairs, pair_width)),
        "q": vmem((length, pairs * pair_width), BF16),
        "k": vmem((length, pairs * pair_width), BF16),
        "v": vmem((length, pairs * pair_width), BF16),
        "do": vmem((length, pairs * pair_width), BF16),
        "log": vmem((2 * pairs, length)),
        "gain": vmem((pairs, pair_width)),
        "load": dma((6,)),
        "store": dma((5, 2)),
        "dq": vmem((length, pairs * pair_width), BF16),
        "dk": vmem((length, pairs * pair_width), BF16),
        "dv": vmem((length, pairs * pair_width), BF16),
        "dlog": vmem((2 * pairs, length)),
        "dgain": vmem((pairs, pair_width)),
        "d_value": vmem((pairs,) + token),
        "d_cum": vmem((2 * pairs, length)),
    }
    kept = [pairs >> (level + 1) for level in range(levels)]
    for name in ("forward", "backward"):
        for level in range(levels):
            for part in ("received", "first", "total", "give"):
                spec[name, part, level] = vmem((kept[level],) + state)
            if level > 0:
                spec[name, "prefix", level] = vmem((kept[level - 1],) + state)
        spec[name, "chain_in"] = vmem((chained,) + state)
        spec[name, "chain_out"] = vmem((chained,) + state)
        for part in ("chain_send", "chain_recv"):
            spec[name, part] = dma((chained,))
        for part in ("up_send", "up_recv", "down_send", "down_recv"):
            spec[name, part] = dma((levels, pairs // 2))
    return spec


def gathered(keys, refs):
    bag = Bag()
    bag.scans = {"forward": Bag(), "backward": Bag()}
    for key, ref in zip(keys, refs):
        if isinstance(key, str):
            setattr(bag, key, ref)
        elif len(key) == 2:
            setattr(bag.scans[key[0]], key[1], ref)
        else:
            scan = bag.scans[key[0]]
            if not hasattr(scan, key[1]):
                setattr(scan, key[1], {})
            getattr(scan, key[1])[key[2]] = ref
    return bag


def shards(size, queries, keys, values, log_decay, gain, d_out):
    seq_size, dp_size, levels = size
    length, features = queries.shape[1:]
    heads = log_decay.shape[1]
    width = features // heads
    pairs = heads // 2
    steps = (seq_size.bit_length() - 1) + (dp_size.bit_length() - 1)
    spec = layout(length, pairs, width, levels, pairs >> levels, steps)
    names = list(spec)

    def body(*refs):
        kernel(size, width, refs[:6], refs[6:11], gathered(names, refs[11:]))

    whole = pl.BlockSpec(memory_space=pltpu.HBM)
    token = jax.ShapeDtypeStruct((length, features), BF16)
    flops = 2 * heads * length * width * (12 * length + 12 * width)
    results = (
        token, token, token,
        jax.ShapeDtypeStruct((heads, length), F32),
        jax.ShapeDtypeStruct((pairs, 2 * width), F32),
    )
    outputs = pl.pallas_call(
        body,
        out_shape=results,
        in_specs=[pl.BlockSpec(memory_space=pltpu.HBM)] * 6,
        out_specs=(whole,) * 5,
        scratch_shapes=list(spec.values()),
        compiler_params=pltpu.CompilerParams(
            collective_id=0, has_side_effects=True, vmem_limit_bytes=VMEM
        ),
        cost_estimate=pl.CostEstimate(
            flops=flops, bytes_accessed=14 * length * features, transcendentals=0
        ),
        name="gated_backward",
    )(queries[0], keys[0], values[0], log_decay[0], gain.reshape(pairs, 2 * width), d_out[0])
    d_queries, d_keys, d_values, d_log_decay, d_gain = pl.pallas_call(
        deliver,
        out_shape=results,
        in_specs=[pl.BlockSpec(memory_space=pl.ANY)] * 5,
        out_specs=(pl.BlockSpec(memory_space=pltpu.HBM),) * 5,
        scratch_shapes=[pltpu.VMEM(r.shape, r.dtype) for r in results]
        + [pltpu.SemaphoreType.DMA((5,))] * 2,
        compiler_params=pltpu.CompilerParams(vmem_limit_bytes=VMEM),
        cost_estimate=pl.CostEstimate(
            flops=0, bytes_accessed=12 * length * features, transcendentals=0
        ),
        name="deliver",
    )(*outputs)
    return d_queries[None], d_keys[None], d_values[None], d_log_decay[None], d_gain.reshape(-1)


def solution(mesh):
    seq_size, dp_size = mesh.shape["seq"], mesh.shape["dp"]
    levels = seq_size.bit_length() // 2
    tokens = P("dp", "seq", None)
    decays = P("dp", None, "seq")
    return jax.shard_map(
        functools.partial(shards, (seq_size, dp_size, levels)),
        mesh=mesh,
        in_specs=(tokens, tokens, tokens, decays, P(), tokens),
        out_specs=(tokens, tokens, tokens, decays, P()),
        check_vma=False,
    )
```

```python
import functools

import jax
import jax.numpy as jnp
from jax import lax
from jax.experimental import pallas as pl
from jax.experimental.pallas import tpu as pltpu
from jax.sharding import PartitionSpec as P

EPSILON = 1e-06
HIGH = lax.Precision.HIGHEST
F32 = jnp.float32
BF16 = jnp.bfloat16
UNROLL = 2
WIDE = 4
VMEM = 58 * 1024 * 1024


def dot(a, b, contract, precision=None):
    return lax.dot_general(
        a, b, (contract, ((), ())), precision=precision, preferred_element_type=F32
    )


def nn(a, b, precision=None):
    return dot(a, b, ((1,), (0,)), precision)


def nt(a, b, precision=None):
    return dot(a, b, ((1,), (1,)), precision)


def tn(a, b):
    return dot(a, b, ((0,), (0,)))


def split(x):
    high = x.astype(BF16)
    return high, (x - high.astype(F32)).astype(BF16)


def rows(*parts):
    return jnp.concatenate(parts, axis=0)


def lanes(*parts):
    return jnp.concatenate(parts, axis=1)


def kernel(
    size,
    width,
    inputs,
    outputs,
    scratch,
):
    s = scratch
    dq_ref, dk_ref, dv_ref, dlog_ref, dgain_ref = s.dq, s.dk, s.dv, s.dlog, s.dgain
    q_ref, k_ref, v_ref, log_ref, gain_ref, do_ref = places = (
        s.q, s.k, s.v, s.log, s.gain, s.do
    )
    loads = [
        pltpu.make_async_copy(source, target, s.load.at[index])
        for index, (source, target) in enumerate(zip(inputs, places))
    ]
    q_load, k_load, v_load, log_load, gain_load, do_load = loads
    for load in (log_load, k_load, v_load, q_load, do_load, gain_load):
        load.start()
    seq_size, dp_size, levels = size
    length = q_ref.shape[0]
    pair_width = 2 * width
    pairs = q_ref.shape[1] // pair_width
    heads = 2 * pairs
    group = 2 ** levels
    chain = seq_size // group
    me = lax.axis_index("seq")
    dp = lax.axis_index("dp")

    def at_seq(index):
        return {"seq": index}

    def bit_of(value, level):
        return lax.rem(lax.div(value, 2 ** level), 2)

    def flipped(value, level):
        return value + 2 ** level * (1 - 2 * bit_of(value, level))

    place = lax.div(me, group)
    after = lax.rem(me + group, seq_size)
    before = lax.rem(me + seq_size - group, seq_size)
    seq_bits = seq_size.bit_length() - 1
    dp_bits = dp_size.bit_length() - 1
    partners = [at_seq(flipped(me, level)) for level in range(seq_bits)]
    partners += [{"dp": flipped(dp, level)} for level in range(dp_bits)]
    greeted = partners + [at_seq(after), at_seq(before)]

    barrier = pltpu.get_barrier_semaphore()
    for other in greeted:
        pl.semaphore_signal(
            barrier, inc=1, device_id=other, device_id_type=pl.DeviceIdType.MESH
        )

    def copy_to(source, target, send, recv, device):
        return pltpu.make_async_remote_copy(
            src_ref=source, dst_ref=target, send_sem=send, recv_sem=recv,
            device_id=device, device_id_type=pl.DeviceIdType.MESH,
        )

    lane_row = lax.broadcasted_iota(jnp.int32, (1, pair_width), 1)
    low_row = lane_row < width

    def low(shape):
        return lax.broadcasted_iota(jnp.int32, shape, 1) < width

    low_tok = low((length, pair_width))
    low_state = low((width, pair_width))

    def columns(pair):
        if isinstance(pair, int):
            return pl.ds(pair * pair_width, pair_width)
        return pl.ds(pl.multiple_of(pair * pair_width, pair_width), pair_width)

    def stacked(block):
        zero = jnp.zeros_like(block)
        return rows(jnp.where(low_tok, block, zero), jnp.where(low_tok, zero, block))

    def diagonal(state):
        zero = jnp.zeros_like(state)
        return rows(jnp.where(low_state, state, zero), jnp.where(low_state, zero, state))

    def packed(square):
        return jnp.where(low_state, square[:width], square[width:])

    upper_sub = lax.broadcasted_iota(jnp.int32, (pair_width, length), 0) < width

    def picked(broad):
        return jnp.where(upper_sub, broad[:, :length], broad[:, length:])

    def each(start, count, compute, unroll=UNROLL):
        if isinstance(count, int) and count % unroll:
            unroll = 1

        def body(index, carry):
            stores = []
            for offset in range(unroll):
                stores += compute(start + index * unroll + offset)
            for ref, where, value in stores:
                ref[where] = value
            return carry

        trips = count // unroll if isinstance(count, int) else lax.div(count, unroll)
        lax.fori_loop(0, trips, body, 0)

    ones_from = lax.broadcasted_iota(jnp.int32, (length, length), 0)
    ones_to = lax.broadcasted_iota(jnp.int32, (length, length), 1)
    causal = ones_from >= ones_to
    log_load.wait()
    log_block = log_ref[...]
    cum_rows = nn(log_block, (ones_from <= ones_to).astype(F32), HIGH)
    s.cum[...] = cum_rows
    s.late_rows[...] = jnp.exp(cum_rows[:, length - 1:length] - cum_rows)
    cum_columns = nt(causal.astype(F32), log_block, HIGH)

    k_load.wait()
    v_load.wait()
    for pair in range(pairs):
        first = jnp.broadcast_to(cum_columns[:, 2 * pair:2 * pair + 1], (length, length))
        second = jnp.broadcast_to(cum_columns[:, 2 * pair + 1:2 * pair + 2], (length, length))
        s.spread[2 * pair] = first
        s.spread[2 * pair + 1] = second
        mixed = jnp.where(low_tok, first, second)
        total = mixed[length - 1:length, :]
        s.grow[pair] = jnp.exp(mixed)
        late = jnp.exp(total - mixed)
        s.late[pair] = late
        s.decay[0, pair:pair + 1, :] = jnp.exp(total)

    def state_of(pair):
        key = k_ref[:, columns(pair)]
        high, rest = split(v_ref[:, columns(pair)].astype(F32) * s.late[pair])
        key_t = jnp.transpose(key)
        fresh = packed(nn(lanes(key_t, key_t), rows(high, rest)))
        return [(s.key_t, pair, key_t), (s.fresh, pair, fresh)]

    pl.semaphore_wait(barrier, len(greeted))

    bits = [bit_of(me, level) for level in range(levels)]
    halves = [pairs >> (level + 1) for level in range(levels)]
    keeps = [bit * half for bit, half in zip(bits, halves)]
    gives = [(1 - bit) * half for bit, half in zip(bits, halves)]
    bases = [0]
    for keep in keeps:
        bases.append(bases[-1] + keep)
    state_shape = (width, pair_width)

    def pieces(level):
        half = halves[level]
        if level == levels - 1:
            return [(i, 1) for i in range(half)]
        return [(gives[level + 1], half // 2), (keeps[level + 1], half // 2)]

    def scan(name, source, result, backward, produce, works, consume):
        x = s.scans[name]
        first_bit = 1 if backward else 0
        owned = [source] + [x.total[level] for level in range(levels)]
        outs = [result] + [x.prefix[level] for level in range(1, levels)]
        mine_first = [jnp.broadcast_to(bit, state_shape) == first_bit for bit in bits]
        row_first = [jnp.broadcast_to(bit, (1, pair_width)) == first_bit for bit in bits]
        partner = [at_seq(flipped(me, level)) for level in range(levels)]

        def up(level, index):
            offset, size = pieces(level)[index]
            return copy_to(
                owned[level].at[pl.ds(gives[level] + offset, size)],
                x.received[level].at[pl.ds(offset, size)],
                x.up_send.at[level, index], x.up_recv.at[level, index], partner[level],
            )

        def decay_copy(level):
            return copy_to(
                s.decay.at[level], s.decay_other.at[level],
                s.decay_send.at[level], s.decay_recv.at[level], partner[level],
            )

        def start_up(level):
            if not backward:
                decay_copy(level).start()
            for index in range(len(pieces(level))):
                up(level, index).start()

        def join(level, index):
            up(level, index).wait_recv()
            offset, size = pieces(level)[index]
            for i in range(size):
                own = owned[level][keeps[level] + offset + i]
                other = x.received[level][offset + i]
                row = pl.ds(bases[level] + keeps[level] + offset + i, 1)
                later_decay = jnp.where(
                    row_first[level], s.decay_other[level, row, :], s.decay[level, row, :]
                )
                earlier = jnp.where(mine_first[level], own, other)
                later = jnp.where(mine_first[level], other, own)
                x.first[level][offset + i] = earlier
                x.total[level][offset + i] = later_decay * earlier + later

        produce(gives[0], halves[0])
        start_up(0)
        produce(keeps[0], halves[0])
        for level in range(levels):
            works[level]()
            if not backward:
                decay_copy(level).wait()
                s.decay[level + 1] = s.decay[level] * s.decay_other[level]
            if level < levels - 1:
                join(level, 0)
                start_up(level + 1)
                join(level, 1)

        start_place = chain - 1 if backward else 0
        stop_place = 0 if backward else chain - 1
        target = at_seq(before if backward else after)
        count = halves[-1]

        def link(i):
            return copy_to(
                x.chain_out.at[i], x.chain_in.at[i],
                x.chain_send.at[i], x.chain_recv.at[i], target,
            )

        def down(level, i):
            place_of = keeps[level] + i
            return copy_to(
                x.give[level].at[i], outs[level].at[place_of],
                x.down_send.at[level, i], x.down_recv.at[level, i], partner[level],
            )

        def arrival(level, i):
            return copy_to(
                x.give[level].at[i], outs[level].at[gives[level] + i],
                x.down_send.at[level, i], x.down_recv.at[level, i], partner[level],
            )

        def descend(level, i, given):
            row = pl.ds(bases[level] + keeps[level] + i, 1)
            first_decay = jnp.where(
                row_first[level], s.decay[level, row, :], s.decay_other[level, row, :]
            )
            moved = first_decay * given + x.first[level][i]
            x.give[level][i] = jnp.where(mine_first[level], moved, given)
            down(level, i).start()
            own = jnp.where(mine_first[level], given, moved)
            outs[level][keeps[level] + i] = own
            if level > 0:
                descend(level - 1, keeps[level] + i, own)

        @pl.when(place == start_place)
        def _():
            x.chain_in[...] = jnp.zeros_like(x.chain_in)

        for i in range(count):
            join(levels - 1, i)
        works[levels]()
        for i in range(count):
            @pl.when(place != start_place)
            def _(i=i):
                link(i).wait_recv()

            @pl.when(place != stop_place)
            def _(i=i):
                row = pl.ds(bases[levels] + i, 1)
                x.chain_out[i] = s.decay[levels, row, :] * x.chain_in[i] + owned[levels][i]
                link(i).start()

            descend(levels - 1, i, x.chain_in[i])
        works[levels + 1]()
        for level in range(levels - 1, 0, -1):
            order = range(halves[level])
            for i in order if level == levels - 1 else ordered(level):
                arrival(level, i).wait_recv()
                descend(level - 1, gives[level] + i, outs[level][gives[level] + i])
        consume(keeps[0], halves[0])
        for i in range(halves[0]):
            arrival(0, i).wait_recv()
        consume(gives[0], halves[0])

        for level in range(levels):
            for index in range(len(pieces(level))):
                up(level, index).wait_send()
            for i in range(halves[level]):
                down(level, i).wait_send()

        @pl.when(place != stop_place)
        def _():
            for i in range(count):
                link(i).wait_send()

    def ordered(level):
        half = halves[level + 1]
        return [keeps[level + 1] + i for i in range(half)] + [
            gives[level + 1] + i for i in range(half)
        ]

    def inside(pair):
        query = q_ref[:, columns(pair)]
        scores = nt(query, stacked(k_ref[:, columns(pair)]))
        tables = []
        for head in range(2):
            gap = s.spread[2 * pair + head] - s.cum[pl.ds(2 * pair + head, 1), :]
            tables.append(jnp.where(causal, jnp.exp(jnp.minimum(gap, 0.0)), 0.0))
        table = lanes(*tables)
        high, rest = split(scores * table)
        values = stacked(v_ref[:, columns(pair)])
        part = nn(lanes(high, rest), rows(values, values))
        return [
            (s.table, pair, table), (s.score_high, pair, high),
            (s.score_rest, pair, rest), (s.attended, pair, part),
            (s.query_t, pair, jnp.transpose(query)),
        ]

    def cut(compute, backward, per_hop):
        distance = chain - 1 - place if backward else place
        waits = (distance > 0).astype(jnp.int32)
        ends = (distance == chain - 1).astype(jnp.int32)
        counts = [2 * waits] + [2 + 2 * waits] * (levels - 1)
        done = 0
        works = []
        for count in counts:
            works.append(functools.partial(each, done, count, compute))
            done = done + count
        left = pairs - done
        middle = jnp.minimum(per_hop * distance, left)
        middle = middle + ends * (left - middle)
        works.append(functools.partial(each, done, middle, compute))
        works.append(functools.partial(each, done + middle, left - middle, compute))
        return works

    s.squares[...] = jnp.zeros_like(s.squares)
    s.products[...] = jnp.zeros_like(s.products)

    def attend(pair):
        query = q_ref[:, columns(pair)]
        high, rest = split(diagonal(s.start[pair]))
        carried = nn(lanes(query, query), rows(high, rest))
        attended = s.attended[pair] + s.grow[pair] * carried
        slope = do_ref[:, columns(pair)].astype(F32) * gain_ref[pl.ds(pair, 1), :]
        return attended, slope

    def attend_range(start, count):
        def body(index, carry):
            squares, products = s.squares[...], s.products[...]
            results = [attend(start + index * WIDE + offset) for offset in range(WIDE)]
            for offset, (attended, slope) in enumerate(results):
                s.attended[start + index * WIDE + offset] = attended
                squares = squares + attended * attended
                products = products + attended * slope
            s.squares[...] = squares
            s.products[...] = products
            return carry

        lax.fori_loop(0, count // WIDE, body, 0)

    q_load.wait()
    arrived = []

    def attend_after_loads(start, count):
        if not arrived:
            gain_load.wait()
            do_load.wait()
            arrived.append(True)
        attend_range(start, count)

    scan(
        "forward", s.fresh, s.start, False,
        lambda start, count: each(start, count, state_of, WIDE),
        cut(inside, False, 4), attend_after_loads,
    )
    features = pairs * pair_width
    mean = jnp.sum(s.squares[...], axis=1, keepdims=True) / features
    inverse = 1.0 / jnp.sqrt(mean + EPSILON)
    weight = jnp.sum(s.products[...], axis=1, keepdims=True) / features * inverse * inverse * inverse
    s.inverse[...] = jnp.broadcast_to(inverse, (length, pair_width))
    s.weight[...] = jnp.broadcast_to(weight, (length, pair_width))

    def slopes(pair):
        cotangent = do_ref[:, columns(pair)].astype(F32)
        attended = s.attended[pair]
        inverse = s.inverse[...]
        gained = jnp.sum(attended * inverse * cotangent, axis=0, keepdims=True)
        slope = cotangent * gain_ref[pl.ds(pair, 1), :] * inverse - attended * s.weight[...]
        high, rest = split(slope)
        grown_high, grown_rest = split(slope * s.grow[pair])
        query_t = s.query_t[pair]
        incoming = packed(nn(lanes(query_t, query_t), rows(grown_high, grown_rest)))
        return [
            (s.slope_high, pair, high), (s.slope_rest, pair, rest),
            (s.incoming, pair, incoming),
            (s.gained, (0, pl.ds(pair, 1), slice(None)), gained),
        ]

    def gain_step(step):
        copy = copy_to(
            s.gained.at[step], s.gained_other.at[step],
            s.gain_send.at[step], s.gain_recv.at[step], partners[step],
        )
        return copy

    def gain_advance(step):
        gain_step(step).wait()
        s.gained[step + 1] = s.gained[step] + s.gained_other[step]
        if step + 1 < len(partners):
            gain_step(step + 1).start()

    def grads(pair):
        query, key = q_ref[:, columns(pair)], k_ref[:, columns(pair)]
        keys, values = stacked(key), stacked(v_ref[:, columns(pair)])
        high, rest = s.slope_high[pair], s.slope_rest[pair]
        from_values = nt(lanes(high, rest), lanes(values, values))
        inner_high, inner_rest = split(from_values * s.table[pair])
        state_high, state_rest = split(diagonal(s.start[pair]))
        carried = nt(lanes(high, rest, high), lanes(state_high, state_high, state_rest))
        d_query = nn(lanes(inner_high, inner_rest), rows(keys, keys)) + s.grow[pair] * carried
        query_t = s.query_t[pair]
        d_key_t = picked(nn(lanes(query_t, query_t), rows(inner_high, inner_rest)))
        score_high, score_rest = s.score_high[pair], s.score_rest[pair]
        high_t, rest_t = jnp.transpose(high), jnp.transpose(rest)
        d_value_t = picked(
            nn(lanes(high_t, high_t, rest_t), rows(score_high, score_rest, score_high))
        )
        change_high, change_rest = split(d_query * query.astype(F32))
        per_head = nt(lanes(sides, sides), lanes(change_high, change_rest))
        return [
            (dq_ref, (slice(None), columns(pair)), d_query.astype(BF16)),
            (s.query_rows, pair, per_head),
            (s.d_key_t, pair, d_key_t), (s.d_value, pair, jnp.transpose(d_value_t)),
        ]

    side_row = lax.broadcasted_iota(jnp.int32, (8, pair_width), 0)
    side_lane = lax.broadcasted_iota(jnp.int32, (8, pair_width), 1)
    sides = (side_row == (side_lane >= width).astype(jnp.int32)).astype(F32).astype(BF16)
    steps = len(partners)

    def with_gain(work, first, last):
        def run():
            work()
            for step in range(first, last):
                gain_advance(step)
        return run

    works = cut(grads, True, 2)
    begun = []

    def produce_slopes(start, count):
        each(start, count, slopes, WIDE)
        begun.append(True)
        if len(begun) == 2:
            gain_step(0).start()

    spread_steps = [steps * i // (levels + 2) for i in range(levels + 3)]
    works = [
        with_gain(work, spread_steps[i], spread_steps[i + 1]) for i, work in enumerate(works)
    ]

    def store(index):
        return pltpu.make_async_copy(results[index], outputs[index], s.store.at[index, 0])

    results = (dq_ref, dk_ref, dv_ref, dlog_ref, dgain_ref)
    stores = []

    s.d_cum[...] = jnp.zeros_like(s.d_cum)
    s.ended[...] = jnp.zeros_like(s.ended)
    head_of = lax.broadcasted_iota(jnp.int32, (heads, pair_width), 0)
    side_of = (lax.broadcasted_iota(jnp.int32, (heads, pair_width), 1) >= width).astype(jnp.int32)

    def finish(pair):
        key, value = k_ref[:, columns(pair)], v_ref[:, columns(pair)]
        end = s.end[pair]
        high, rest = split(diagonal(end))
        late_t = jnp.where(
            upper_sub, s.late_rows[pl.ds(2 * pair, 1), :], s.late_rows[pl.ds(2 * pair + 1, 1), :]
        )
        d_key_t = s.d_key_t[pair] + late_t * nt(lanes(high, rest), lanes(value, value))
        d_value = s.d_value[pair] + s.late[pair] * nn(lanes(key, key), rows(high, rest))
        change = d_key_t * s.key_t[pair].astype(F32)
        first = s.query_rows[pair, 0:1] - jnp.sum(change[:width], axis=0, keepdims=True)
        second = s.query_rows[pair, 1:2] - jnp.sum(change[width:], axis=0, keepdims=True)
        d_cum = jnp.where(head_of == 2 * pair, first, 0.0)
        d_cum = jnp.where(head_of == 2 * pair + 1, second, d_cum)
        last_state = s.decay[0, pl.ds(pair, 1), :] * s.start[pair] + s.fresh[pair]
        ended = jnp.sum(last_state * end, axis=0, keepdims=True)
        ended = jnp.where(head_of == 2 * pair + side_of, ended, 0.0)
        return jnp.transpose(d_key_t.astype(BF16)), d_value.astype(BF16), d_cum, ended

    def finish_range(start, count):
        if not stores:
            dgain_ref[...] = s.gained[steps]
            begin = [store(0), store(4)]
            for copy in begin:
                copy.start()
            stores.extend(begin)

        def body(index, carry):
            total, ends = s.d_cum[...], s.ended[...]
            results = [finish(start + index * WIDE + offset) for offset in range(WIDE)]
            for offset, (d_key, d_value, d_cum, ended) in enumerate(results):
                pair = start + index * WIDE + offset
                dk_ref[:, columns(pair)] = d_key
                dv_ref[:, columns(pair)] = d_value
                total = total + d_cum
                ends = ends + ended
            s.d_cum[...] = total
            s.ended[...] = ends
            return carry

        lax.fori_loop(0, count // WIDE, body, 0)
        where = pl.ds(pl.multiple_of(start * pair_width, pair_width), count * pair_width)
        slot = len(stores) // 4
        for index in (1, 2):
            copy = pltpu.make_async_copy(
                results[index].at[:, where], outputs[index].at[:, where], s.store.at[index, slot]
            )
            copy.start()
            stores.append(copy)

    scan("backward", s.incoming, s.end, True, produce_slopes, works, finish_range)
    through = jnp.sum(s.ended[...], axis=1, keepdims=True)
    dlog_ref[...] = nn(s.d_cum[...], causal.astype(F32), HIGH) + through
    stores.append(store(3))
    stores[-1].start()
    for copy in stores:
        copy.wait()


def deliver(*refs):
    sources, targets, held, (read, wrote) = refs[:5], refs[5:10], refs[10:15], refs[15:]
    reads = [
        pltpu.make_async_copy(source, place, read.at[index])
        for index, (source, place) in enumerate(zip(sources, held))
    ]
    writes = [
        pltpu.make_async_copy(place, target, wrote.at[index])
        for index, (place, target) in enumerate(zip(held, targets))
    ]
    for copy in reads:
        copy.start()
    for copy, following in zip(reads, writes):
        copy.wait()
        following.start()
    for copy in writes:
        copy.wait()


class Bag:
    pass


def layout(length, pairs, width, levels, chained, steps):
    pair_width = 2 * width
    state = (width, pair_width)
    token = (length, pair_width)
    wide = (length, 2 * length)
    dma = pltpu.SemaphoreType.DMA

    def vmem(shape, dtype=F32):
        return pltpu.VMEM(shape, dtype)

    spec = {
        "cum": vmem((2 * pairs, length)),
        "spread": vmem((2 * pairs, length, length)),
        "grow": vmem((pairs,) + token),
        "late": vmem((pairs,) + token),
        "decay": vmem((levels + 1, pairs, pair_width)),
        "decay_other": vmem((levels, pairs, pair_width)),
        "decay_send": dma((levels,)),
        "decay_recv": dma((levels,)),
        "fresh": vmem((pairs,) + state),
        "start": vmem((pairs,) + state),
        "incoming": vmem((pairs,) + state),
        "end": vmem((pairs,) + state),
        "table": vmem((pairs,) + wide),
        "score_high": vmem((pairs,) + wide, BF16),
        "score_rest": vmem((pairs,) + wide, BF16),
        "attended": vmem((pairs,) + token),
        "squares": vmem(token),
        "products": vmem(token),
        "inverse": vmem(token),
        "weight": vmem(token),
        "slope_high": vmem((pairs,) + token, BF16),
        "slope_rest": vmem((pairs,) + token, BF16),
        "gained": vmem((steps + 1, pairs, pair_width)),
        "gained_other": vmem((steps, pairs, pair_width)),
        "gain_send": dma((steps,)),
        "gain_recv": dma((steps,)),
        "query_rows": vmem((pairs, 8, length)),
        "query_t": vmem((pairs, pair_width, length), BF16),
        "key_t": vmem((pairs, pair_width, length), BF16),
        "late_rows": vmem((2 * pairs, length)),
        "d_key_t": vmem((pairs, pair_width, length)),
        "ended": vmem((2 * pairs, pair_width)),
        "q": vmem((length, pairs * pair_width), BF16),
        "k": vmem((length, pairs * pair_width), BF16),
        "v": vmem((length, pairs * pair_width), BF16),
        "do": vmem((length, pairs * pair_width), BF16),
        "log": vmem((2 * pairs, length)),
        "gain": vmem((pairs, pair_width)),
        "load": dma((6,)),
        "store": dma((5, 2)),
        "dq": vmem((length, pairs * pair_width), BF16),
        "dk": vmem((length, pairs * pair_width), BF16),
        "dv": vmem((length, pairs * pair_width), BF16),
        "dlog": vmem((2 * pairs, length)),
        "dgain": vmem((pairs, pair_width)),
        "d_value": vmem((pairs,) + token),
        "d_cum": vmem((2 * pairs, length)),
    }
    kept = [pairs >> (level + 1) for level in range(levels)]
    for name in ("forward", "backward"):
        for level in range(levels):
            for part in ("received", "first", "total", "give"):
                spec[name, part, level] = vmem((kept[level],) + state)
            if level > 0:
                spec[name, "prefix", level] = vmem((kept[level - 1],) + state)
        spec[name, "chain_in"] = vmem((chained,) + state)
        spec[name, "chain_out"] = vmem((chained,) + state)
        for part in ("chain_send", "chain_recv"):
            spec[name, part] = dma((chained,))
        for part in ("up_send", "up_recv", "down_send", "down_recv"):
            spec[name, part] = dma((levels, pairs // 2))
    return spec


def gathered(keys, refs):
    bag = Bag()
    bag.scans = {"forward": Bag(), "backward": Bag()}
    for key, ref in zip(keys, refs):
        if isinstance(key, str):
            setattr(bag, key, ref)
        elif len(key) == 2:
            setattr(bag.scans[key[0]], key[1], ref)
        else:
            scan = bag.scans[key[0]]
            if not hasattr(scan, key[1]):
                setattr(scan, key[1], {})
            getattr(scan, key[1])[key[2]] = ref
    return bag


def shards(size, queries, keys, values, log_decay, gain, d_out):
    seq_size, dp_size, levels = size
    length, features = queries.shape[1:]
    heads = log_decay.shape[1]
    width = features // heads
    pairs = heads // 2
    steps = (seq_size.bit_length() - 1) + (dp_size.bit_length() - 1)
    spec = layout(length, pairs, width, levels, pairs >> levels, steps)
    names = list(spec)

    def body(*refs):
        kernel(size, width, refs[:6], refs[6:11], gathered(names, refs[11:]))

    whole = pl.BlockSpec(memory_space=pltpu.HBM)
    token = jax.ShapeDtypeStruct((length, features), BF16)
    flops = 2 * heads * length * width * (12 * length + 12 * width)
    results = (
        token, token, token,
        jax.ShapeDtypeStruct((heads, length), F32),
        jax.ShapeDtypeStruct((pairs, 2 * width), F32),
    )
    outputs = pl.pallas_call(
        body,
        out_shape=results,
        in_specs=[pl.BlockSpec(memory_space=pltpu.HBM)] * 6,
        out_specs=(whole,) * 5,
        scratch_shapes=list(spec.values()),
        compiler_params=pltpu.CompilerParams(
            collective_id=0, has_side_effects=True, vmem_limit_bytes=VMEM
        ),
        cost_estimate=pl.CostEstimate(
            flops=flops, bytes_accessed=14 * length * features, transcendentals=0
        ),
        name="gated_backward",
    )(queries[0], keys[0], values[0], log_decay[0], gain.reshape(pairs, 2 * width), d_out[0])
    d_queries, d_keys, d_values, d_log_decay, d_gain = pl.pallas_call(
        deliver,
        out_shape=results,
        in_specs=[pl.BlockSpec(memory_space=pl.ANY)] * 5,
        out_specs=(pl.BlockSpec(memory_space=pltpu.HBM),) * 5,
        scratch_shapes=[pltpu.VMEM(r.shape, r.dtype) for r in results]
        + [pltpu.SemaphoreType.DMA((5,))] * 2,
        compiler_params=pltpu.CompilerParams(vmem_limit_bytes=VMEM),
        cost_estimate=pl.CostEstimate(
            flops=0, bytes_accessed=12 * length * features, transcendentals=0
        ),
        name="deliver",
    )(*outputs)
    return d_queries[None], d_keys[None], d_values[None], d_log_decay[None], d_gain.reshape(-1)


def solution(mesh):
    seq_size, dp_size = mesh.shape["seq"], mesh.shape["dp"]
    levels = seq_size.bit_length() // 2
    tokens = P("dp", "seq", None)
    decays = P("dp", None, "seq")
    return jax.shard_map(
        functools.partial(shards, (seq_size, dp_size, levels)),
        mesh=mesh,
        in_specs=(tokens, tokens, tokens, decays, P(), tokens),
        out_specs=(tokens, tokens, tokens, decays, P()),
        check_vma=False,
    )
```

```python
import functools

import jax
import jax.numpy as jnp
from jax import lax
from jax.experimental import pallas as pl
from jax.experimental.pallas import tpu as pltpu
from jax.sharding import PartitionSpec as P

EPSILON = 1e-06
HIGH = lax.Precision.HIGHEST
F32 = jnp.float32
BF16 = jnp.bfloat16
UNROLL = 2
WIDE = 4
VMEM = 52 * 1024 * 1024


def dot(a, b, contract, precision=None):
    return lax.dot_general(
        a, b, (contract, ((), ())), precision=precision, preferred_element_type=F32
    )


def nn(a, b, precision=None):
    return dot(a, b, ((1,), (0,)), precision)


def nt(a, b, precision=None):
    return dot(a, b, ((1,), (1,)), precision)


def tn(a, b):
    return dot(a, b, ((0,), (0,)))


def split(x):
    high = x.astype(BF16)
    return high, (x - high.astype(F32)).astype(BF16)


def rows(*parts):
    return jnp.concatenate(parts, axis=0)


def lanes(*parts):
    return jnp.concatenate(parts, axis=1)


def kernel(
    size,
    width,
    inputs,
    outputs,
    scratch,
):
    s = scratch
    dq_ref, dk_ref, dv_ref, dlog_ref, dgain_ref = s.dq, s.dk, s.dv, s.dlog, s.dgain
    q_ref, k_ref, v_ref, log_ref, gain_ref, do_ref = places = (
        s.q, s.k, s.v, s.log, s.gain, s.do
    )
    loads = [
        pltpu.make_async_copy(source, target, s.load.at[index])
        for index, (source, target) in enumerate(zip(inputs, places))
    ]
    q_load, k_load, v_load, log_load, gain_load, do_load = loads
    for load in (log_load, k_load, v_load, q_load, do_load, gain_load):
        load.start()
    seq_size, dp_size, levels = size
    length = q_ref.shape[0]
    pair_width = 2 * width
    pairs = q_ref.shape[1] // pair_width
    heads = 2 * pairs
    group = 2 ** levels
    chain = seq_size // group
    me = lax.axis_index("seq")
    dp = lax.axis_index("dp")

    def at_seq(index):
        return {"seq": index}

    def bit_of(value, level):
        return lax.rem(lax.div(value, 2 ** level), 2)

    def flipped(value, level):
        return value + 2 ** level * (1 - 2 * bit_of(value, level))

    place = lax.div(me, group)
    after = lax.rem(me + group, seq_size)
    before = lax.rem(me + seq_size - group, seq_size)
    seq_bits = seq_size.bit_length() - 1
    dp_bits = dp_size.bit_length() - 1
    partners = [at_seq(flipped(me, level)) for level in range(seq_bits)]
    partners += [{"dp": flipped(dp, level)} for level in range(dp_bits)]
    greeted = partners + [at_seq(after), at_seq(before)]

    barrier = pltpu.get_barrier_semaphore()
    for other in greeted:
        pl.semaphore_signal(
            barrier, inc=1, device_id=other, device_id_type=pl.DeviceIdType.MESH
        )

    def copy_to(source, target, send, recv, device):
        return pltpu.make_async_remote_copy(
            src_ref=source, dst_ref=target, send_sem=send, recv_sem=recv,
            device_id=device, device_id_type=pl.DeviceIdType.MESH,
        )

    lane_row = lax.broadcasted_iota(jnp.int32, (1, pair_width), 1)
    low_row = lane_row < width

    def low(shape):
        return lax.broadcasted_iota(jnp.int32, shape, 1) < width

    low_tok = low((length, pair_width))
    low_state = low((width, pair_width))

    def columns(pair):
        if isinstance(pair, int):
            return pl.ds(pair * pair_width, pair_width)
        return pl.ds(pl.multiple_of(pair * pair_width, pair_width), pair_width)

    def stacked(block):
        zero = jnp.zeros_like(block)
        return rows(jnp.where(low_tok, block, zero), jnp.where(low_tok, zero, block))

    def diagonal(state):
        zero = jnp.zeros_like(state)
        return rows(jnp.where(low_state, state, zero), jnp.where(low_state, zero, state))

    def packed(square):
        return jnp.where(low_state, square[:width], square[width:])

    upper_sub = lax.broadcasted_iota(jnp.int32, (pair_width, length), 0) < width

    def picked(broad):
        return jnp.where(upper_sub, broad[:, :length], broad[:, length:])

    def each(start, count, compute, unroll=UNROLL):
        if isinstance(count, int) and count % unroll:
            unroll = 1

        def body(index, carry):
            stores = []
            for offset in range(unroll):
                stores += compute(start + index * unroll + offset)
            for ref, where, value in stores:
                ref[where] = value
            return carry

        trips = count // unroll if isinstance(count, int) else lax.div(count, unroll)
        lax.fori_loop(0, trips, body, 0)

    ones_from = lax.broadcasted_iota(jnp.int32, (length, length), 0)
    ones_to = lax.broadcasted_iota(jnp.int32, (length, length), 1)
    causal = ones_from >= ones_to
    log_load.wait()
    log_block = log_ref[...]
    cum_rows = nn(log_block, (ones_from <= ones_to).astype(F32), HIGH)
    s.cum[...] = cum_rows
    s.late_rows[...] = jnp.exp(cum_rows[:, length - 1:length] - cum_rows)
    cum_columns = nt(causal.astype(F32), log_block, HIGH)

    for pair in range(pairs):
        first = jnp.broadcast_to(cum_columns[:, 2 * pair:2 * pair + 1], (length, length))
        second = jnp.broadcast_to(cum_columns[:, 2 * pair + 1:2 * pair + 2], (length, length))
        s.spread[2 * pair] = first
        s.spread[2 * pair + 1] = second
        mixed = jnp.where(low_tok, first, second)
        total = mixed[length - 1:length, :]
        s.late[pair] = jnp.exp(total - mixed)
        s.decay[0, pair:pair + 1, :] = jnp.exp(total)

    def state_of(pair):
        key = k_ref[:, columns(pair)]
        high, rest = split(v_ref[:, columns(pair)].astype(F32) * s.late[pair])
        key_t = jnp.transpose(key)
        fresh = packed(nn(lanes(key_t, key_t), rows(high, rest)))
        return [(s.key_t, pair, key_t), (s.fresh, pair, fresh)]

    k_load.wait()
    v_load.wait()
    pl.semaphore_wait(barrier, len(greeted))

    bits = [bit_of(me, level) for level in range(levels)]
    halves = [pairs >> (level + 1) for level in range(levels)]
    keeps = [bit * half for bit, half in zip(bits, halves)]
    gives = [(1 - bit) * half for bit, half in zip(bits, halves)]
    bases = [0]
    for keep in keeps:
        bases.append(bases[-1] + keep)
    state_shape = (width, pair_width)

    def pieces(level):
        half = halves[level]
        if level == levels - 1:
            return [(i, 1) for i in range(half)]
        return [(gives[level + 1], half // 2), (keeps[level + 1], half // 2)]

    def scan(name, source, result, backward, produce, works, consume):
        x = s.scans[name]
        first_bit = 1 if backward else 0
        owned = [source] + [x.total[level] for level in range(levels)]
        outs = [result] + [x.prefix[level] for level in range(1, levels)]
        mine_first = [jnp.broadcast_to(bit, state_shape) == first_bit for bit in bits]
        row_first = [jnp.broadcast_to(bit, (1, pair_width)) == first_bit for bit in bits]
        partner = [at_seq(flipped(me, level)) for level in range(levels)]

        def up(level, index):
            offset, size = pieces(level)[index]
            return copy_to(
                owned[level].at[pl.ds(gives[level] + offset, size)],
                x.received[level].at[pl.ds(offset, size)],
                x.up_send.at[level, index], x.up_recv.at[level, index], partner[level],
            )

        def decay_copy(level):
            return copy_to(
                s.decay.at[level], s.decay_other.at[level],
                s.decay_send.at[level], s.decay_recv.at[level], partner[level],
            )

        def start_up(level):
            if not backward:
                decay_copy(level).start()
            for index in range(len(pieces(level))):
                up(level, index).start()

        def join(level, index):
            up(level, index).wait_recv()
            offset, size = pieces(level)[index]
            for i in range(size):
                own = owned[level][keeps[level] + offset + i]
                other = x.received[level][offset + i]
                row = pl.ds(bases[level] + keeps[level] + offset + i, 1)
                later_decay = jnp.where(
                    row_first[level], s.decay_other[level, row, :], s.decay[level, row, :]
                )
                earlier = jnp.where(mine_first[level], own, other)
                later = jnp.where(mine_first[level], other, own)
                x.first[level][offset + i] = earlier
                x.total[level][offset + i] = later_decay * earlier + later

        for index, (offset, size) in enumerate(pieces(0)):
            produce(gives[0] + offset, size)
            if index == 0 and not backward:
                decay_copy(0).start()
            up(0, index).start()
        offset, size = pieces(0)[0]
        produce(keeps[0] + offset, size)
        for level in range(levels):
            if level > 0:
                works[level]()
            if not backward:
                decay_copy(level).wait()
                s.decay[level + 1] = s.decay[level] * s.decay_other[level]
            if level < levels - 1:
                join(level, 0)
                start_up(level + 1)
                if level == 0:
                    offset, size = pieces(0)[1]
                    produce(keeps[0] + offset, size)
                    works[0]()
                join(level, 1)

        start_place = chain - 1 if backward else 0
        stop_place = 0 if backward else chain - 1
        target = at_seq(before if backward else after)
        count = halves[-1]

        def link(i):
            return copy_to(
                x.chain_out.at[i], x.chain_in.at[i],
                x.chain_send.at[i], x.chain_recv.at[i], target,
            )

        def down(level, i):
            place_of = keeps[level] + i
            return copy_to(
                x.give[level].at[i], outs[level].at[place_of],
                x.down_send.at[level, i], x.down_recv.at[level, i], partner[level],
            )

        def arrival(level, i):
            return copy_to(
                x.give[level].at[i], outs[level].at[gives[level] + i],
                x.down_send.at[level, i], x.down_recv.at[level, i], partner[level],
            )

        def descend(level, i, given):
            row = pl.ds(bases[level] + keeps[level] + i, 1)
            first_decay = jnp.where(
                row_first[level], s.decay[level, row, :], s.decay_other[level, row, :]
            )
            moved = first_decay * given + x.first[level][i]
            x.give[level][i] = jnp.where(mine_first[level], moved, given)
            down(level, i).start()
            own = jnp.where(mine_first[level], given, moved)
            outs[level][keeps[level] + i] = own
            if level > 0:
                descend(level - 1, keeps[level] + i, own)

        @pl.when(place == start_place)
        def _():
            x.chain_in[...] = jnp.zeros_like(x.chain_in)

        for i in range(count):
            join(levels - 1, i)
        works[levels]()
        for i in range(count):
            @pl.when(place != start_place)
            def _(i=i):
                link(i).wait_recv()

            @pl.when(place != stop_place)
            def _(i=i):
                row = pl.ds(bases[levels] + i, 1)
                x.chain_out[i] = s.decay[levels, row, :] * x.chain_in[i] + owned[levels][i]
                link(i).start()

            descend(levels - 1, i, x.chain_in[i])
        works[levels + 1]()
        for level in range(levels - 1, 0, -1):
            order = range(halves[level])
            for i in order if level == levels - 1 else ordered(level):
                arrival(level, i).wait_recv()
                descend(level - 1, gives[level] + i, outs[level][gives[level] + i])
        consume(keeps[0], halves[0])
        for i in range(halves[0]):
            arrival(0, i).wait_recv()
        consume(gives[0], halves[0])

        for level in range(levels):
            for index in range(len(pieces(level))):
                up(level, index).wait_send()
            for i in range(halves[level]):
                down(level, i).wait_send()

        @pl.when(place != stop_place)
        def _():
            for i in range(count):
                link(i).wait_send()

    def ordered(level):
        half = halves[level + 1]
        return [keeps[level + 1] + i for i in range(half)] + [
            gives[level + 1] + i for i in range(half)
        ]

    def inside(pair):
        query = q_ref[:, columns(pair)]
        grow = jnp.exp(jnp.where(low_tok, s.spread[2 * pair], s.spread[2 * pair + 1]))
        scores = nt(query, stacked(k_ref[:, columns(pair)]))
        tables = []
        for head in range(2):
            gap = s.spread[2 * pair + head] - s.cum[pl.ds(2 * pair + head, 1), :]
            tables.append(jnp.where(causal, jnp.exp(jnp.minimum(gap, 0.0)), 0.0))
        table = lanes(*tables)
        high, rest = split(scores * table)
        values = stacked(v_ref[:, columns(pair)])
        part = nn(lanes(high, rest), rows(values, values))
        return [
            (s.table, pair, table), (s.score_high, pair, high),
            (s.score_rest, pair, rest), (s.attended, pair, part),
            (s.query_t, pair, jnp.transpose(query)), (s.grow, pair, grow),
        ]

    def cut(compute, backward, per_hop):
        distance = chain - 1 - place if backward else place
        waits = (distance > 0).astype(jnp.int32)
        ends = (distance == chain - 1).astype(jnp.int32)
        counts = [2 * waits] + [2 + 2 * waits] * (levels - 1)
        done = 0
        works = []
        for count in counts:
            works.append(functools.partial(each, done, count, compute))
            done = done + count
        left = pairs - done
        middle = jnp.minimum(per_hop * distance, left)
        middle = middle + ends * (left - middle)
        works.append(functools.partial(each, done, middle, compute))
        works.append(functools.partial(each, done + middle, left - middle, compute))
        return works

    s.squares[...] = jnp.zeros_like(s.squares)
    s.products[...] = jnp.zeros_like(s.products)

    def attend(pair):
        query = q_ref[:, columns(pair)]
        high, rest = split(diagonal(s.start[pair]))
        carried = nn(lanes(query, query), rows(high, rest))
        attended = s.attended[pair] + s.grow[pair] * carried
        slope = do_ref[:, columns(pair)].astype(F32) * gain_ref[pl.ds(pair, 1), :]
        return attended, slope

    def attend_range(start, count):
        def body(index, carry):
            squares, products = s.squares[...], s.products[...]
            results = [attend(start + index * WIDE + offset) for offset in range(WIDE)]
            for offset, (attended, slope) in enumerate(results):
                s.attended[start + index * WIDE + offset] = attended
                squares = squares + attended * attended
                products = products + attended * slope
            s.squares[...] = squares
            s.products[...] = products
            return carry

        lax.fori_loop(0, count // WIDE, body, 0)

    q_load.wait()
    arrived = []

    def attend_after_loads(start, count):
        if not arrived:
            gain_load.wait()
            do_load.wait()
            arrived.append(True)
        attend_range(start, count)

    scan(
        "forward", s.fresh, s.start, False,
        lambda start, count: each(start, count, state_of, WIDE),
        cut(inside, False, 4), attend_after_loads,
    )
    features = pairs * pair_width
    mean = jnp.sum(s.squares[...], axis=1, keepdims=True) / features
    inverse = 1.0 / jnp.sqrt(mean + EPSILON)
    weight = jnp.sum(s.products[...], axis=1, keepdims=True) / features * inverse * inverse * inverse
    s.inverse[...] = jnp.broadcast_to(inverse, (length, pair_width))
    s.weight[...] = jnp.broadcast_to(weight, (length, pair_width))

    def slopes(pair):
        cotangent = do_ref[:, columns(pair)].astype(F32)
        attended = s.attended[pair]
        inverse = s.inverse[...]
        gained = jnp.sum(attended * inverse * cotangent, axis=0, keepdims=True)
        slope = cotangent * gain_ref[pl.ds(pair, 1), :] * inverse - attended * s.weight[...]
        high, rest = split(slope)
        grown_high, grown_rest = split(slope * s.grow[pair])
        query_t = s.query_t[pair]
        incoming = packed(nn(lanes(query_t, query_t), rows(grown_high, grown_rest)))
        return [
            (s.slope_high, pair, high), (s.slope_rest, pair, rest),
            (s.incoming, pair, incoming),
            (s.gained, (0, pl.ds(pair, 1), slice(None)), gained),
        ]

    def gain_step(step):
        copy = copy_to(
            s.gained.at[step], s.gained_other.at[step],
            s.gain_send.at[step], s.gain_recv.at[step], partners[step],
        )
        return copy

    def gain_advance(step):
        gain_step(step).wait()
        s.gained[step + 1] = s.gained[step] + s.gained_other[step]
        if step + 1 < len(partners):
            gain_step(step + 1).start()

    def grads(pair):
        query, key = q_ref[:, columns(pair)], k_ref[:, columns(pair)]
        keys, values = stacked(key), stacked(v_ref[:, columns(pair)])
        high, rest = s.slope_high[pair], s.slope_rest[pair]
        from_values = nt(lanes(high, rest), lanes(values, values))
        inner_high, inner_rest = split(from_values * s.table[pair])
        state_high, state_rest = split(diagonal(s.start[pair]))
        carried = nt(lanes(high, rest, high), lanes(state_high, state_high, state_rest))
        d_query = nn(lanes(inner_high, inner_rest), rows(keys, keys)) + s.grow[pair] * carried
        query_t = s.query_t[pair]
        d_key_t = picked(nn(lanes(query_t, query_t), rows(inner_high, inner_rest)))
        score_high, score_rest = s.score_high[pair], s.score_rest[pair]
        high_t, rest_t = jnp.transpose(high), jnp.transpose(rest)
        d_value_t = picked(
            nn(lanes(high_t, high_t, rest_t), rows(score_high, score_rest, score_high))
        )
        change_high, change_rest = split(d_query * query.astype(F32))
        per_head = nt(lanes(sides, sides), lanes(change_high, change_rest))
        return [
            (dq_ref, (slice(None), columns(pair)), d_query.astype(BF16)),
            (s.query_rows, pair, per_head),
            (s.d_key_t, pair, d_key_t), (s.d_value, pair, jnp.transpose(d_value_t)),
        ]

    side_row = lax.broadcasted_iota(jnp.int32, (8, pair_width), 0)
    side_lane = lax.broadcasted_iota(jnp.int32, (8, pair_width), 1)
    sides = (side_row == (side_lane >= width).astype(jnp.int32)).astype(F32).astype(BF16)
    steps = len(partners)

    def with_gain(work, first, last):
        def run():
            work()
            for step in range(first, last):
                gain_advance(step)
        return run

    works = cut(grads, True, 2)
    begun = []

    def produce_slopes(start, count):
        each(start, count, slopes, WIDE)
        begun.append(True)
        if len(begun) == 4:
            gain_step(0).start()

    spread_steps = [0] + [steps * i // (levels + 1) for i in range(levels + 2)]
    works = [
        with_gain(work, spread_steps[i], spread_steps[i + 1]) for i, work in enumerate(works)
    ]

    def store(index):
        return pltpu.make_async_copy(results[index], outputs[index], s.store.at[index, 0])

    results = (dq_ref, dk_ref, dv_ref, dlog_ref, dgain_ref)
    stores = []

    s.d_cum[...] = jnp.zeros_like(s.d_cum)
    s.ended[...] = jnp.zeros_like(s.ended)
    head_of = lax.broadcasted_iota(jnp.int32, (heads, pair_width), 0)
    side_of = (lax.broadcasted_iota(jnp.int32, (heads, pair_width), 1) >= width).astype(jnp.int32)

    def finish(pair):
        key, value = k_ref[:, columns(pair)], v_ref[:, columns(pair)]
        end = s.end[pair]
        high, rest = split(diagonal(end))
        late_t = jnp.where(
            upper_sub, s.late_rows[pl.ds(2 * pair, 1), :], s.late_rows[pl.ds(2 * pair + 1, 1), :]
        )
        d_key_t = s.d_key_t[pair] + late_t * nt(lanes(high, rest), lanes(value, value))
        d_value = s.d_value[pair] + s.late[pair] * nn(lanes(key, key), rows(high, rest))
        change = d_key_t * s.key_t[pair].astype(F32)
        first = s.query_rows[pair, 0:1] - jnp.sum(change[:width], axis=0, keepdims=True)
        second = s.query_rows[pair, 1:2] - jnp.sum(change[width:], axis=0, keepdims=True)
        d_cum = jnp.where(head_of == 2 * pair, first, 0.0)
        d_cum = jnp.where(head_of == 2 * pair + 1, second, d_cum)
        last_state = s.decay[0, pl.ds(pair, 1), :] * s.start[pair] + s.fresh[pair]
        ended = jnp.sum(last_state * end, axis=0, keepdims=True)
        ended = jnp.where(head_of == 2 * pair + side_of, ended, 0.0)
        return jnp.transpose(d_key_t.astype(BF16)), d_value.astype(BF16), d_cum, ended

    def finish_range(start, count):
        if not stores:
            dgain_ref[...] = s.gained[steps]
            begin = [store(0), store(4)]
            for copy in begin:
                copy.start()
            stores.extend(begin)

        def body(index, carry):
            total, ends = s.d_cum[...], s.ended[...]
            results = [finish(start + index * WIDE + offset) for offset in range(WIDE)]
            for offset, (d_key, d_value, d_cum, ended) in enumerate(results):
                pair = start + index * WIDE + offset
                dk_ref[:, columns(pair)] = d_key
                dv_ref[:, columns(pair)] = d_value
                total = total + d_cum
                ends = ends + ended
            s.d_cum[...] = total
            s.ended[...] = ends
            return carry

        lax.fori_loop(0, count // WIDE, body, 0)
        where = pl.ds(pl.multiple_of(start * pair_width, pair_width), count * pair_width)
        slot = len(stores) // 4
        for index in (1, 2):
            copy = pltpu.make_async_copy(
                results[index].at[:, where], outputs[index].at[:, where], s.store.at[index, slot]
            )
            copy.start()
            stores.append(copy)

    scan("backward", s.incoming, s.end, True, produce_slopes, works, finish_range)
    through = jnp.sum(s.ended[...], axis=1, keepdims=True)
    dlog_ref[...] = nn(s.d_cum[...], causal.astype(F32), HIGH) + through
    stores.append(store(3))
    stores[-1].start()
    for copy in stores:
        copy.wait()


def deliver(*refs):
    sources, targets, done = refs[:5], refs[5:10], refs[10]
    copies = [
        pltpu.make_async_copy(source, target, done.at[index])
        for index, (source, target) in enumerate(zip(sources, targets))
    ]
    for copy in copies:
        copy.start()
    for copy in copies:
        copy.wait()


class Bag:
    pass


def layout(length, pairs, width, levels, chained, steps):
    pair_width = 2 * width
    state = (width, pair_width)
    token = (length, pair_width)
    wide = (length, 2 * length)
    dma = pltpu.SemaphoreType.DMA

    def vmem(shape, dtype=F32):
        return pltpu.VMEM(shape, dtype)

    spec = {
        "cum": vmem((2 * pairs, length)),
        "spread": vmem((2 * pairs, length, length)),
        "grow": vmem((pairs,) + token),
        "late": vmem((pairs,) + token),
        "decay": vmem((levels + 1, pairs, pair_width)),
        "decay_other": vmem((levels, pairs, pair_width)),
        "decay_send": dma((levels,)),
        "decay_recv": dma((levels,)),
        "fresh": vmem((pairs,) + state),
        "start": vmem((pairs,) + state),
        "incoming": vmem((pairs,) + state),
        "end": vmem((pairs,) + state),
        "table": vmem((pairs,) + wide),
        "score_high": vmem((pairs,) + wide, BF16),
        "score_rest": vmem((pairs,) + wide, BF16),
        "attended": vmem((pairs,) + token),
        "squares": vmem(token),
        "products": vmem(token),
        "inverse": vmem(token),
        "weight": vmem(token),
        "slope_high": vmem((pairs,) + token, BF16),
        "slope_rest": vmem((pairs,) + token, BF16),
        "gained": vmem((steps + 1, pairs, pair_width)),
        "gained_other": vmem((steps, pairs, pair_width)),
        "gain_send": dma((steps,)),
        "gain_recv": dma((steps,)),
        "query_rows": vmem((pairs, 8, length)),
        "query_t": vmem((pairs, pair_width, length), BF16),
        "key_t": vmem((pairs, pair_width, length), BF16),
        "late_rows": vmem((2 * pairs, length)),
        "d_key_t": vmem((pairs, pair_width, length)),
        "ended": vmem((2 * pairs, pair_width)),
        "q": vmem((length, pairs * pair_width), BF16),
        "k": vmem((length, pairs * pair_width), BF16),
        "v": vmem((length, pairs * pair_width), BF16),
        "do": vmem((length, pairs * pair_width), BF16),
        "log": vmem((2 * pairs, length)),
        "gain": vmem((pairs, pair_width)),
        "load": dma((6,)),
        "store": dma((5, 2)),
        "dq": vmem((length, pairs * pair_width), BF16),
        "dk": vmem((length, pairs * pair_width), BF16),
        "dv": vmem((length, pairs * pair_width), BF16),
        "dlog": vmem((2 * pairs, length)),
        "dgain": vmem((pairs, pair_width)),
        "d_value": vmem((pairs,) + token),
        "d_cum": vmem((2 * pairs, length)),
    }
    kept = [pairs >> (level + 1) for level in range(levels)]
    for name in ("forward", "backward"):
        for level in range(levels):
            for part in ("received", "first", "total", "give"):
                spec[name, part, level] = vmem((kept[level],) + state)
            if level > 0:
                spec[name, "prefix", level] = vmem((kept[level - 1],) + state)
        spec[name, "chain_in"] = vmem((chained,) + state)
        spec[name, "chain_out"] = vmem((chained,) + state)
        for part in ("chain_send", "chain_recv"):
            spec[name, part] = dma((chained,))
        for part in ("up_send", "up_recv", "down_send", "down_recv"):
            spec[name, part] = dma((levels, pairs // 2))
    return spec


def gathered(keys, refs):
    bag = Bag()
    bag.scans = {"forward": Bag(), "backward": Bag()}
    for key, ref in zip(keys, refs):
        if isinstance(key, str):
            setattr(bag, key, ref)
        elif len(key) == 2:
            setattr(bag.scans[key[0]], key[1], ref)
        else:
            scan = bag.scans[key[0]]
            if not hasattr(scan, key[1]):
                setattr(scan, key[1], {})
            getattr(scan, key[1])[key[2]] = ref
    return bag


def shards(size, queries, keys, values, log_decay, gain, d_out):
    seq_size, dp_size, levels = size
    length, features = queries.shape[1:]
    heads = log_decay.shape[1]
    width = features // heads
    pairs = heads // 2
    steps = (seq_size.bit_length() - 1) + (dp_size.bit_length() - 1)
    spec = layout(length, pairs, width, levels, pairs >> levels, steps)
    names = list(spec)

    def body(*refs):
        kernel(size, width, refs[:6], refs[6:11], gathered(names, refs[11:]))

    whole = pl.BlockSpec(memory_space=pl.ANY)
    token = jax.ShapeDtypeStruct((length, features), BF16)
    flops = 2 * heads * length * width * (12 * length + 12 * width)
    results = (
        token, token, token,
        jax.ShapeDtypeStruct((heads, length), F32),
        jax.ShapeDtypeStruct((pairs, 2 * width), F32),
    )
    outputs = pl.pallas_call(
        body,
        out_shape=results,
        in_specs=[pl.BlockSpec(memory_space=pltpu.HBM)] * 6,
        out_specs=(whole,) * 5,
        scratch_shapes=list(spec.values()),
        compiler_params=pltpu.CompilerParams(
            collective_id=0, has_side_effects=True, vmem_limit_bytes=VMEM
        ),
        cost_estimate=pl.CostEstimate(
            flops=flops, bytes_accessed=14 * length * features, transcendentals=0
        ),
        name="gated_backward",
    )(queries[0], keys[0], values[0], log_decay[0], gain.reshape(pairs, 2 * width), d_out[0])
    d_queries, d_keys, d_values, d_log_decay, d_gain = pl.pallas_call(
        deliver,
        out_shape=results,
        in_specs=[pl.BlockSpec(memory_space=pl.ANY)] * 5,
        out_specs=(pl.BlockSpec(memory_space=pltpu.HBM),) * 5,
        scratch_shapes=[pltpu.SemaphoreType.DMA((5,))],
        cost_estimate=pl.CostEstimate(
            flops=0, bytes_accessed=12 * length * features, transcendentals=0
        ),
        name="deliver",
    )(*outputs)
    return d_queries[None], d_keys[None], d_values[None], d_log_decay[None], d_gain.reshape(-1)


def solution(mesh):
    seq_size, dp_size = mesh.shape["seq"], mesh.shape["dp"]
    levels = seq_size.bit_length() // 2
    tokens = P("dp", "seq", None)
    decays = P("dp", None, "seq")
    return jax.shard_map(
        functools.partial(shards, (seq_size, dp_size, levels)),
        mesh=mesh,
        in_specs=(tokens, tokens, tokens, decays, P(), tokens),
        out_specs=(tokens, tokens, tokens, decays, P()),
        check_vma=False,
    )
```
